32 devices in a mesh: batch: 8 (over z, y), chan: 4 (over x, core).
Axes of the slice: x: 2, y: 2, z: 4, core: 2. Of those that a mesh axis runs over, the one named last changes fastest.
Arguments:
- features: bfloat16 [512, 16384], P('chan', 'batch'), may hold values from -6 to 6
- time_emb: bfloat16 [16, 1024], P('batch', 'chan'), may hold values from -6 to 6
- labels: int32 [16], P('batch'), may hold values from 0 to 999
- extents: int32 [16, 2], P('batch'), may hold values from 16 to 32, as said below
- cotangent: bfloat16 [512, 16384], P('chan', 'batch'), may hold values from -6 to 6
- gn1_gain: float32 [512], P('chan'), may hold values from 0.5 to 1.5
- gn1_bias: float32 [512], P('chan'), may hold values from -3 to 3
- conv1_w: bfloat16 [9, 512, 512], P(None, 'chan'), may hold values from -0.09375 to 0.09375
- conv1_b: float32 [512], P('chan'), may hold values from -3 to 3
- emb_w: bfloat16 [1024, 2, 512], P(None, None, 'chan'), may hold values from -0.1875 to 0.1875
- emb_b: float32 [2, 512], P(None, 'chan'), may hold values from -2 to 2
- gn2_gain: float32 [512], P('chan'), may hold values from 0.5 to 1.5
- gn2_bias: float32 [512], P('chan'), may hold values from -3 to 3
- conv2_w: bfloat16 [9, 512, 512], P(None, None, 'chan'), may hold values from -0.09375 to 0.09375
- conv2_b: float32 [512], P('chan'), may hold values from -3 to 3
- gn3_gain: float32 [512], P('chan'), may hold values from 0.5 to 1.5
- gn3_bias: float32 [512], P('chan'), may hold values from -3 to 3
- qkv_w: bfloat16 [3, 512, 512], P(None, 'chan'), may hold values from -0.25 to 0.25
- qkv_b: float32 [2, 512], P(None, 'chan'), may hold values from -3 to 3
- proj_w: bfloat16 [512, 512], P(None, 'chan'), may hold values from -3 to 3
- proj_b: float32 [512], P('chan'), may hold values from -3 to 3
- class_table: bfloat16 [1000, 1024], P(None, 'chan'), may hold values from -6 to 6
Outputs:
- output: bfloat16 [512, 16384], P('chan', 'batch')
- features_grad: float32 [512, 16384], P('chan', 'batch')
- time_grad: float32 [16, 1024], P('batch', 'chan')
- gn1_gain_grad: float32 [512], P('chan')
- gn1_bias_grad: float32 [512], P('chan')
- conv1_w_grad: float32 [9, 512, 512], P(None, 'chan')
- conv1_b_grad: float32 [512], P('chan')
- emb_w_grad: float32 [1024, 2, 512], P(None, None, 'chan')
- emb_b_grad: float32 [2, 512], P(None, 'chan')
- gn2_gain_grad: float32 [512], P('chan')
- gn2_bias_grad: float32 [512], P('chan')
- conv2_w_grad: float32 [9, 512, 512], P(None, None, 'chan')
- conv2_b_grad: float32 [512], P('chan')
- gn3_gain_grad: float32 [512], P('chan')
- gn3_bias_grad: float32 [512], P('chan')
- qkv_w_grad: float32 [3, 512, 512], P(None, 'chan')
- qkv_b_grad: float32 [2, 512], P(None, 'chan')
- proj_w_grad: float32 [512, 512], P(None, 'chan')
- proj_b_grad: float32 [512], P('chan')
- class_table_grad: float32 [1000, 1024], P(None, 'chan')
The draws below stay inside these ranges and needn't reach their ends.
Inputs may be any that keep to these rules, and one draw needn't show every extreme that they name: Each image's valid region is its top-left extents[i, 0] rows by extents[i, 1] columns; in every draw some image has both extents 32 and another has both 32 // 2.
All inputs are finite; a program needn't handle non-finite values.
Results may differ from the reference program's by a relative error of at most 0.029.
Values may be sent and summed in bfloat16 or wider, within the bound.
No kernel may reach another device: no remote copies, remote signals or barrier semaphores. Data moves between devices by JAX's collectives and lax.ppermute only.
A program may use at most 192 MiB of HBM per device.

```python
import math
import jax
import jax.numpy as jnp
from jax import lax

C = 512
HEAD_DIM = 64
GROUPS = 32
EMB = 1024
CLASSES = 1000
SIDE = 32
HEADS = 8
IMAGES = 16
PIXELS = 16384


def draw_extents(key, part):
    key = jax.random.fold_in(key, 11)
    key_sizes, key_widest, key_offset = jax.random.split(key, 3)
    drawn = jax.random.randint(key_sizes, (IMAGES, 2), SIDE // 2, SIDE + 1, dtype=jnp.int32)
    widest = jax.random.randint(key_widest, (), 0, IMAGES, dtype=jnp.int32)
    offset = jax.random.randint(key_offset, (), 1, IMAGES, dtype=jnp.int32)
    narrowest = (widest + offset) % IMAGES
    drawn = drawn.at[widest].set(SIDE)
    drawn = drawn.at[narrowest].set(SIDE // 2)
    return drawn


def place_ends(result, stream_key, smallest, high):
    place = [jax.random.randint(jax.random.fold_in(stream_key, axis), (), 0, length) for axis, length in enumerate(result.shape)]
    widest = result.shape.index(max(result.shape))
    beside = place[:widest] + [(place[widest] + 1) % result.shape[widest]] + place[widest + 1:]
    return result.at[tuple(place)].set(smallest).at[tuple(beside)].set(high)


def shard_levels(stream_key, dims, cuts, smallest, largest):
    gain = 1.0
    for position, parts in cuts:
        steps = jax.random.uniform(jax.random.fold_in(jax.random.fold_in(stream_key, 6), position), (parts,), jnp.float32, smallest / len(cuts), largest / len(cuts))
        gain = gain * jnp.repeat(jnp.exp(steps), dims[position] // parts).reshape((-1,) + (1,) * (len(dims) - 1 - position))
    return gain


def scatter_about(own_key, dims, deviation, limit, cuts=(), held_as=jnp.bfloat16):
    entries = deviation * jax.random.normal(own_key, dims, jnp.float32)
    if cuts:
        entries = entries * shard_levels(own_key, dims, cuts, -0.22, 0.18)
    return jnp.clip(entries, -limit, limit).astype(held_as)


def setup_inputs(seed: int = 0) -> dict:
    splits = jax.random.split(jax.random.key(seed), 23)
    return {
        "features": scatter_about(splits[0], (C, PIXELS), 1.0, 6.0, ((0, 4), (1, 8))),
        "time_emb": scatter_about(splits[1], (IMAGES, EMB), 1.0, 6.0, ((0, 8), (1, 4))),
        "labels": place_ends(jax.random.randint(splits[2], (IMAGES,), 0, CLASSES), jax.random.fold_in(splits[2], 1), 0, CLASSES - 1).astype(jnp.int32),
        "extents": draw_extents(jax.random.fold_in(splits[22], 71), 0),
        "cotangent": scatter_about(splits[4], (C, PIXELS), 1.0, 6.0, ((0, 4), (1, 8))),
        "gn1_gain": jnp.clip(1.0 + 0.1 * jax.random.normal(splits[5], (C,), jnp.float32), 0.5, 1.5),
        "gn1_bias": scatter_about(splits[6], (C,), 0.5, 3.0, ((0, 4),), jnp.float32),
        "conv1_w": scatter_about(splits[7], (9, C, C), (9 * C) ** -0.5, 0.09375, ((1, 4),)),
        "conv1_b": scatter_about(splits[8], (C,), 0.5, 3.0, ((0, 4),), jnp.float32),
        "emb_w": scatter_about(splits[9], (EMB, 2, C), EMB ** -0.5, 0.1875, ((2, 4),)),
        "emb_b": scatter_about(splits[10], (2, C), 0.3, 2.0, ((1, 4),), jnp.float32),
        "gn2_gain": jnp.clip(1.0 + 0.1 * jax.random.normal(splits[11], (C,), jnp.float32), 0.5, 1.5),
        "gn2_bias": scatter_about(splits[12], (C,), 0.5, 3.0, ((0, 4),), jnp.float32),
        "conv2_w": scatter_about(splits[13], (9, C, C), (9 * C) ** -0.5, 0.09375, ((2, 4),)),
        "conv2_b": scatter_about(splits[14], (C,), 0.5, 3.0, ((0, 4),), jnp.float32),
        "gn3_gain": jnp.clip(1.0 + 0.1 * jax.random.normal(splits[15], (C,), jnp.float32), 0.5, 1.5),
        "gn3_bias": scatter_about(splits[16], (C,), 0.5, 3.0, ((0, 4),), jnp.float32),
        "qkv_w": scatter_about(splits[17], (3, C, C), C ** -0.5, 0.25, ((1, 4),)),
        "qkv_b": scatter_about(splits[18], (2, C), 0.5, 3.0, ((1, 4),), jnp.float32),
        "proj_w": scatter_about(splits[19], (C, C), 4 ** -0.5, 3.0, ((1, 4),)),
        "proj_b": scatter_about(splits[20], (C,), 0.5, 3.0, ((0, 4),), jnp.float32),
        "class_table": scatter_about(splits[21], (CLASSES, EMB), 1.0, 6.0, ((1, 4),)),
    }


@jax.custom_vjp
def low(v):
    return lax.optimization_barrier(v.astype(jnp.bfloat16)).astype(jnp.float32)

@jax.custom_vjp
def low_back(v):
    return v

def low_keep(v):
    return (low(v), None)

def low_pass(kept, grad):
    return (grad,)

def back_keep(v):
    return (v, None)

def back_low(kept, grad):
    return (low(grad),)
low.defvjp(low_keep, low_pass)
low_back.defvjp(back_keep, back_low)
highest = lax.Precision.HIGHEST

def valid_mask(extents):
    places = jnp.arange(SIDE, dtype=jnp.int32)
    inside = (places[None, :, None] < extents[:, 0][:, None, None]) & (places[None, None, :] < extents[:, 1][:, None, None])
    return inside.reshape(extents.shape[0], SIDE * SIDE).astype(jnp.float32)

def group_norm(values, gain_vec, bias_vec, valid):
    channels, images, pixels = values.shape
    group_width = C // GROUPS
    grouped = values.reshape(channels // group_width, group_width, images, pixels)
    weight_mask = valid[None, None, :, :]
    counted = group_width * lax.optimization_barrier(jnp.sum(valid, axis=1))
    center = lax.optimization_barrier(jnp.sum(grouped * weight_mask, axis=(1, 3))) / counted
    deviate = grouped - center[:, None, :, None]
    spread = lax.optimization_barrier(jnp.sum(deviate * deviate * weight_mask, axis=(1, 3))) / counted
    normal = deviate * lax.rsqrt(spread + 1e-05)[:, None, :, None]
    return normal.reshape(channels, images, pixels) * gain_vec[:, None, None] + bias_vec[:, None, None]

def shifted(values, direction):
    channels = values.shape[0]
    grid = values.reshape(channels, -1, SIDE, SIDE)
    padded = jnp.pad(grid, ((0, 0), (0, 0), (1, 1), (1, 1)))
    stacked = []
    for row_step in (-1, 0, 1):
        for col_step in (-1, 0, 1):
            row_start = 1 + direction * row_step
            col_start = 1 + direction * col_step
            stacked.append(padded[:, :, row_start:row_start + SIDE, col_start:col_start + SIDE].reshape(channels, -1))
    return jnp.stack(stacked)

def attend_image(inputs):
    queries, key_vecs, values, valid_row = inputs
    scores = jnp.einsum('hcp,hct->hpt', queries, key_vecs, precision=highest) * (1.0 / math.sqrt(HEAD_DIM))
    scores = low_back(scores)
    masked = jnp.where(valid_row[None, None, :] > 0, scores, -1e+30)
    row_peak = lax.optimization_barrier(jnp.max(masked, axis=-1, keepdims=True))
    exponent = jnp.exp(masked - row_peak)
    weights = low(exponent / lax.optimization_barrier(jnp.sum(exponent, axis=-1, keepdims=True)))
    return jnp.einsum('hpt,hct->hcp', weights, values, precision=highest)

def reference(features, time_emb, labels, extents, cotangent, gn1_gain, gn1_bias, conv1_w, conv1_b, emb_w, emb_b, gn2_gain, gn2_bias, conv2_w, conv2_b, gn3_gain, gn3_bias, qkv_w, qkv_b, proj_w, proj_b, class_table):
    pixels = SIDE * SIDE
    images = extents.shape[0]
    valid = valid_mask(extents)
    onehot = (labels[:, None] == jnp.arange(CLASSES, dtype=jnp.int32)[None, :]).astype(jnp.float32)

    def convolve(activations, weight):
        return jnp.einsum('koi,kip->op', weight, shifted(activations, 1), precision=highest)

    def to_images(values):
        return values.reshape(values.shape[0], images, pixels)

    def to_heads(values):
        return values.reshape(HEADS, HEAD_DIM, images, pixels).transpose(2, 0, 1, 3)

    def forward(feat_f, time_vec, norm1_gain, norm1_bias, conv1_weight, conv1_bias, embed_weight, embed_bias, norm2_gain, norm2_bias, conv2_weight, conv2_bias, norm3_gain, norm3_bias, attn_weight, attn_bias, proj_weight, proj_bias, table_vec):
        act_one = low(jax.nn.silu(group_norm(to_images(feat_f), norm1_gain, norm1_bias, valid)).reshape(C, -1))
        hidden = low_back(convolve(act_one, conv1_weight) + conv1_bias[:, None])
        embedding = time_vec + jnp.dot(onehot, table_vec, precision=highest)
        embed_act = low(jax.nn.silu(embedding))
        embed_out = low_back(jnp.dot(embed_act, embed_weight.reshape(EMB, 2 * C), precision=highest).reshape(images, 2, C) + embed_bias[None])
        scale_term = jnp.transpose(embed_out[:, 0, :])[:, :, None]
        shift_term = jnp.transpose(embed_out[:, 1, :])[:, :, None]
        modulated = group_norm(to_images(hidden), norm2_gain, norm2_bias, valid) * (1.0 + scale_term) + shift_term
        act_two = low(jax.nn.silu(modulated).reshape(C, -1))
        middle = feat_f + low_back(convolve(act_two, conv2_weight) + conv2_bias[:, None])
        normed = low(group_norm(to_images(middle), norm3_gain, norm3_bias, valid).reshape(C, -1))
        projected = jnp.einsum('joi,ip->jop', attn_weight, normed, precision=highest)
        queries = low(low_back(projected[0] + attn_bias[0][:, None]))
        key_vecs = low(low_back(projected[1]))
        values = low(low_back(projected[2] + attn_bias[1][:, None]))
        attended = lax.map(jax.checkpoint(attend_image), (to_heads(queries), to_heads(key_vecs), to_heads(values), valid))
        attended = low(low_back(attended.transpose(1, 2, 0, 3).reshape(C, -1)))
        return middle + low_back(jnp.dot(proj_weight, attended, precision=highest) + proj_bias[:, None])
    output, pullback = jax.vjp(forward, features.astype(jnp.float32), time_emb.astype(jnp.float32), gn1_gain, gn1_bias, conv1_w.astype(jnp.float32), conv1_b, emb_w.astype(jnp.float32), emb_b, gn2_gain, gn2_bias, conv2_w.astype(jnp.float32), conv2_b, gn3_gain, gn3_bias, qkv_w.astype(jnp.float32), qkv_b, proj_w.astype(jnp.float32), proj_b, class_table.astype(jnp.float32))
    grads = pullback(cotangent.astype(jnp.float32))
    return (output.astype(jnp.bfloat16), grads[0], grads[1], grads[2], grads[3], grads[4], grads[5], grads[6], grads[7], grads[8], grads[9], grads[10], grads[11], grads[12], grads[13], grads[14], grads[15], grads[16], grads[17], grads[18])
```

```python
import jax
import jax.numpy as jnp
import numpy as np
from jax import lax
from jax.experimental import pallas as pl
from jax.experimental.pallas import tpu as pltpu
from jax.sharding import PartitionSpec as P

CLASSES = 1000
SIDE = 32
PIX = SIDE * SIDE
BLK = 128
HEAD = 64
HALF = BLK // 2
WIDTH = 16
TAPS = 9
BF = jnp.bfloat16
F32 = jnp.float32
highest = lax.Precision.HIGHEST

GN1G, GN1B, C1B, GN2G, GN2B, C2B, GN3G, GN3B, QB, VB, PB, EMB0 = range(12)


def call(kernel, name, inputs, outs, scratch=(), after=(), us=2.0):
    smem = pl.BlockSpec(memory_space=pltpu.SMEM)
    vmem = pl.BlockSpec(memory_space=pltpu.VMEM)
    specs = [smem if value.dtype == jnp.int32 else vmem for value in inputs]
    specs += [pl.BlockSpec(memory_space=pl.ANY)] * len(after)
    first, last = len(inputs), len(inputs) + len(after)

    def body_of(*refs):
        kernel(*refs[:first], *refs[last:])

    return pl.pallas_call(
        body_of,
        name=name,
        out_shape=[jax.ShapeDtypeStruct(shape, dtype) for shape, dtype in outs],
        in_specs=specs,
        out_specs=[vmem] * len(outs),
        scratch_shapes=[pltpu.VMEM(shape, dtype) for shape, dtype in scratch],
        compiler_params=pltpu.CompilerParams(vmem_limit_bytes=MIB[name] * 2**20),
        cost_estimate=pl.CostEstimate(
            flops=0, bytes_accessed=int(us * COST_PER_US), transcendentals=0
        ),
    )(*inputs, *after)


COST_PER_US = 3_000_000
MIB = dict(
    embed=64,
    near=64,
    modulate=6,
    front=24,
    second_conv=16,
    pair_sum=4,
    flip=8,
    middle=12,
    attend=32,
    project=10,
    middle_back=12,
    attend_weights=12,
    back_own=24,
    back_oth=28,
    output=8,
    conv1_own=20,
    conv1_oth=20,
    act_back=16,
    act_sum=8,
    embed_back=6,
    embed_across=4,
    features_back=12,
    collect=4,
    finish=4,
    place_conv1=10,
    place_conv2=10,
    place_attend=8,
)


def dot(lhs, rhs):
    return jnp.dot(lhs, rhs, preferred_element_type=F32)


def dot_nt(lhs, rhs):
    return lax.dot_general(lhs, rhs, (((1,), (1,)), ((), ())), preferred_element_type=F32)


def loop(count, step):
    def body_of(index, carry):
        step(index)
        return carry

    lax.fori_loop(0, count, body_of, 0)


def window(index, size):
    return pl.ds(pl.multiple_of(index * size, size), size)


def pixel_rows():
    place = lax.broadcasted_iota(jnp.int32, (1, PIX), 1)
    return place >> 5, place & (SIDE - 1)


def image_index(ids, other):
    return (ids[0] >> 1) ^ other


def extent(ids, image, axis):
    return ids[2 + 2 * image + axis]


def valid_row(ids, image):
    row, col = pixel_rows()
    inside = (row < extent(ids, image, 0)) & (col < extent(ids, image, 1))
    return jnp.where(inside, 1.0, 0.0).astype(F32)


def counted(ids, image):
    return (WIDTH * extent(ids, image, 0) * extent(ids, image, 1)).astype(F32)


def normalize(values, mask, count):
    channels = values.shape[0]
    grouped = values.reshape(channels // WIDTH, WIDTH, PIX)
    weight = mask.reshape(1, 1, PIX)
    center = jnp.sum(grouped * weight, axis=(1, 2), keepdims=True) / count
    deviate = grouped - center
    spread = jnp.sum(deviate * deviate * weight, axis=(1, 2), keepdims=True) / count
    scale = lax.rsqrt(spread + 1e-05)
    normal = (deviate * scale).reshape(channels, PIX)
    spread_out = jnp.broadcast_to(scale, (channels // WIDTH, WIDTH, BLK)).reshape(channels, BLK)
    return normal, spread_out


def group_total(column):
    channels = column.shape[0]
    wide = jnp.broadcast_to(column, (channels, BLK)).reshape(channels // WIDTH, WIDTH, BLK)
    summed = jnp.sum(wide, axis=1, keepdims=True)
    return jnp.broadcast_to(summed, wide.shape).reshape(channels, BLK)[:, :1]


def norm_back(upstream, normal, scale, mask, count, gain):
    with_norm = jnp.sum(upstream * normal, axis=1, keepdims=True)
    plain = jnp.sum(upstream, axis=1, keepdims=True)
    first = group_total(gain * plain) / count
    second = group_total(gain * with_norm) / count
    back = scale * (gain * upstream - mask * (first + normal * second))
    return back, with_norm, plain


def silu(value):
    half = 0.5 * value
    return half + half * jnp.tanh(half)


def silu_slope(value):
    gate = 0.5 + 0.5 * jnp.tanh(0.5 * value)
    return gate * (1.0 + value * (1.0 - gate))


def move_rows(value, step):
    row, _ = pixel_rows()
    moved = pltpu.roll(value, (-SIDE * step) % PIX, 1)
    return jnp.where((row + step >= 0) & (row + step < SIDE), moved, 0.0)


def move_cols(value, step):
    _, col = pixel_rows()
    moved = pltpu.roll(value, (-step) % PIX, 1)
    return jnp.where((col + step >= 0) & (col + step < SIDE), moved, 0.0)


def tap_start(row_step, col_step):
    return (3 * (row_step + 1) + col_step + 1) * BLK


def tap_rows(row_step, col_step):
    start = tap_start(row_step, col_step)
    return slice(start, start + BLK)


def shift_sum(parts, direction):
    total = None
    for col_step in (-1, 0, 1):
        column = parts[tap_rows(0, col_step), :]
        for row_step in (-1, 1):
            column = column + move_rows(parts[tap_rows(row_step, col_step), :], direction * row_step)
        if col_step:
            column = move_cols(column, direction * col_step)
        total = column if total is None else total + column
    return total


def shift_stack(value, stack, direction):
    whole = value[...].astype(F32)
    for row_step in (-1, 0, 1):
        row_moved = whole if row_step == 0 else move_rows(whole, direction * row_step)
        for col_step in (-1, 0, 1):
            moved = row_moved if col_step == 0 else move_cols(row_moved, direction * col_step)
            stack[tap_rows(row_step, col_step), :] = moved.astype(BF)


def block_rows(place, bit):
    return pl.ds(pl.multiple_of((place ^ bit) * BLK, BLK), BLK)


def image_lanes(image):
    return pl.ds(pl.multiple_of(image * PIX, PIX), PIX)


def columns_of(rows):
    return jnp.transpose(rows)


def side_by_side(columns):
    channels = columns[0].shape[0]
    lane = lax.broadcasted_iota(jnp.int32, (channels, BLK), 1)
    wide = jnp.zeros((channels, BLK), F32)
    for index, column in enumerate(columns):
        wide = jnp.where(lane == index, column, wide)
    return wide


def embed_kernel(
    ids,
    labels,
    time_emb,
    table,
    g1,
    b1,
    c1,
    g2,
    b2,
    c2,
    g3,
    b3,
    qvb,
    pb,
    qkv,
    proj,
    cot,
    pack,
    embedding,
    crossing,
    cot_cols,
):
    for part in range(2):
        start = image_index(ids, 1) * PIX + part * PIX // 2
        crossing[(2 + part) * BLK : (3 + part) * BLK, :] = cot[
            :, pl.ds(pl.multiple_of(start, PIX // 2), PIX // 2)
        ]
    cot_cols[...] = jnp.broadcast_to(
        jnp.sum(cot[...].astype(F32), axis=1, keepdims=True), (BLK, BLK)
    )

    @pl.when((ids[1] & 1) == 0)
    def _():
        crossing[:BLK, :] = qkv[0]
        crossing[BLK : 2 * BLK, :] = qkv[1]

    @pl.when((ids[1] & 1) == 1)
    def _():
        crossing[:BLK, :] = qkv[2]
        crossing[BLK : 2 * BLK, :] = jnp.transpose(proj[...])

    width = time_emb.shape[1]
    for row, ref in enumerate((g1, b1, c1, g2, b2, c2, g3, b3)):
        pack[row : row + 1, :] = ref[...]
    pack[QB : QB + 2, :] = qvb[...]
    pack[PB : PB + 1, :] = pb[...]
    pack[EMB0 + 4 :, :] = jnp.zeros((1, BLK), F32)
    kind = lax.broadcasted_iota(jnp.int32, (16, CLASSES), 1)
    row = lax.broadcasted_iota(jnp.int32, (16, CLASSES), 0)
    label = jnp.where(row == 0, labels[0], labels[1])
    rows = dot(jnp.where((kind == label) & (row < 2), 1.0, 0.0).astype(BF), table[...])
    total = time_emb[...].astype(F32) + rows[:2]
    embedding[...] = total
    act = silu(total).astype(BF).astype(F32)
    for image in range(2):
        for part in range(width // BLK):
            place = EMB0 + image * (width // BLK) + part
            pack[place : place + 1, :] = act[
                image : image + 1, part * BLK : (part + 1) * BLK
            ]


def first_act(feat, cols, mask, count):
    normal, _ = normalize(feat.astype(F32), mask, count)
    return silu(normal * cols[:, GN1G : GN1G + 1] + cols[:, GN1B : GN1B + 1]).astype(BF)


def near_kernel(ids, f0, f1, p0, p1, acts):
    for block, (feat, pack) in enumerate(((f0, p0), (f1, p1))):
        cols = columns_of(pack[...])

        def step(image):
            lanes = image_lanes(image)
            acts[block * BLK : (block + 1) * BLK, lanes] = first_act(
                feat[:, lanes], cols, valid_row(ids, image), counted(ids, image)
            )

        loop(2, step)


def modulate_kernel(ids, p0, p1, p2, p3, emb_w, emb_b, pack, mod, emb_full):
    for bit, ref in enumerate((p0, p1, p2, p3)):
        pack[bit] = ref[...]
    width = emb_full.shape[1] // 4
    emb_full[...] = jnp.zeros(emb_full.shape, F32)
    for bit in range(4):
        for image in range(2):
            for part in range(width // BLK):
                row = EMB0 + image * (width // BLK) + part
                lanes = pl.ds(pl.multiple_of((ids[0] ^ bit) * width + part * BLK, BLK), BLK)
                emb_full[image : image + 1, lanes] = pack[bit, row : row + 1, :]
    made = dot(emb_full[...].astype(BF), emb_w[...])
    mod[...] = jnp.zeros(mod.shape, F32)
    for image in range(2):
        for kind in range(2):
            mod[image, kind : kind + 1, :] = (
                made[image : image + 1, kind * BLK : (kind + 1) * BLK] + emb_b[kind : kind + 1, :]
            )


def front_kernel(other):
    def kernel(
        ids, near, f2, f3, pack, mod_ref, w1, act1, nrm2, scale2, act2, parts, hidden
    ):
        place = ids[0]
        image = image_index(ids, other)
        lanes = image_lanes(image)
        mask = valid_row(ids, image)
        count = counted(ids, image)
        for bit in (0, 1):
            act1[block_rows(place, bit), :] = near[bit * BLK : (bit + 1) * BLK, lanes]
        hidden[0] = f2[:, lanes].astype(F32)
        hidden[1] = f3[:, lanes].astype(F32)

        def first(block):
            cols = columns_of(pack[2 + block])
            act1[block_rows(place, 2 + block), :] = first_act(hidden[block], cols, mask, count)

        loop(2, first)
        parts[...] = dot(w1[...], act1[...])
        cols = columns_of(pack[0])
        normal, scale = normalize(shift_sum(parts, 1) + cols[:, C1B : C1B + 1], mask, count)
        nrm2[...] = normal
        scale2[...] = scale
        mod = columns_of(mod_ref[image])
        plain = normal * cols[:, GN2G : GN2G + 1] + cols[:, GN2B : GN2B + 1]
        act2[...] = silu(plain * (1.0 + mod[:, 0:1]) + mod[:, 1:2]).astype(BF)

    return kernel


def second_conv_kernel(ids, w2, act2, keep, g0, g1, g2, g3, stack, w2_rows):
    place = ids[0]
    for slot, bit in enumerate((0, 2, 1, 3)):
        for tap in range(TAPS):
            w2_rows[slot * BLK : (slot + 1) * BLK, tap * BLK : (tap + 1) * BLK] = w2[
                tap, block_rows(place, bit), :
            ]
    shift_stack(act2, stack, 1)
    made = dot(w2_rows[...], stack[...])
    keep[...] = made[: 2 * BLK].astype(keep.dtype)
    for index, give in enumerate((g0, g1, g2, g3)):
        start = 2 * BLK + index * HALF
        give[...] = made[start : start + HALF].astype(BF)


def pair_sum_kernel(keep, b0, b1, b2, b3, out):
    for index, beside in enumerate((b0, b1, b2, b3)):
        rows = slice(index * HALF, (index + 1) * HALF)
        out[rows, :] = (keep[rows, :].astype(F32) + beside[...].astype(F32)).astype(BF)


def flip_kernel(ids, w1, w2, w1t, w2t):
    place = ids[0]

    def step(tap):
        lanes = window(tap, BLK)
        for slot, bit in enumerate((0, 2, 1, 3)):
            block = w1[tap, :, block_rows(place, bit)]
            w1t[slot * BLK : (slot + 1) * BLK, lanes] = jnp.transpose(block)
        w2t[lanes, :] = jnp.transpose(w2[tap])

    loop(TAPS, step)


def middle_kernel(
    ids, keep, b0, b1, b2, b3, across, f0, f2, pack, middle, normed0, normed1
):
    image = image_index(ids, 0)
    mask = valid_row(ids, image)
    count = counted(ids, image)
    feats = (f0[:, image_lanes(image)], f2[:, image_lanes(image)])
    for index, (feat, pieces, bit, normed) in enumerate(
        zip(feats, ((b0, b1), (b2, b3)), (0, 2), (normed0, normed1))
    ):
        rows = slice(index * BLK, (index + 1) * BLK)
        other = slice((1 - index) * BLK, (2 - index) * BLK)
        cols = columns_of(pack[bit])
        beside = jnp.concatenate([piece[...].astype(F32) for piece in pieces], axis=0)
        total = keep[rows, :] + beside + across[other, :].astype(F32)
        total = feat.astype(F32) + (total + cols[:, C2B : C2B + 1])
        middle[rows, :] = total
        normal, _ = normalize(total, mask, count)
        normed[...] = (normal * cols[:, GN3G : GN3G + 1] + cols[:, GN3B : GN3B + 1]).astype(BF)


BLOCK = 512


def attend_kernel(
    ids,
    norm0,
    norm1,
    norm2,
    norm3,
    c0,
    c1,
    c2,
    c3,
    pack,
    wq_own,
    wp_own,
    half_x,
    half_y,
    norm_full,
    cot_full,
    attended,
    grads,
    keep_norm,
    give_norm0,
    give_norm1,
    heads,
    total,
    bias,
    grad_kt,
    grad_vt,
    wq_back,
    wp_back,
    across,
):
    place = ids[0]
    image = image_index(ids, 0)
    mine = ids[1] & 1
    across[mine] = half_x[...]
    across[1 - mine] = half_y[...]
    wq_across = across[...].reshape(4 * BLK, 4 * BLK)
    for bit, ref in enumerate((norm0, norm1, norm2, norm3)):
        norm_full[block_rows(place, bit), :] = ref[...]
    for bit, ref in enumerate((c0, c1)):
        cot_full[block_rows(place, bit), :] = ref[:, image_lanes(image)]
    for bit, ref in enumerate((c2, c3)):
        for part in range(2):
            lanes = slice(part * PIX // 2, (part + 1) * PIX // 2)
            cot_full[block_rows(place, bit + 2), lanes] = ref[part * BLK : (part + 1) * BLK, :]
    cols_own = columns_of(pack[0])
    cols_across = columns_of(pack[2])
    own = wq_own[...].reshape(3 * BLK, 4 * BLK)
    for index, (weight, proj, cols) in enumerate(
        (
            (own, jnp.transpose(wp_own[...]), cols_own),
            (wq_across[: 3 * BLK], wq_across[3 * BLK :], cols_across),
        )
    ):
        rows = slice(index * BLK, (index + 1) * BLK)
        made = dot(weight, norm_full[...])
        query = (made[:BLK] + cols[:, QB : QB + 1]).astype(BF)
        heads[0, rows, :] = (query.astype(F32) * (1.0 / HEAD**0.5)).astype(BF)
        heads[1, rows, :] = made[BLK : 2 * BLK].astype(BF)
        heads[2, rows, :] = (made[2 * BLK :] + cols[:, VB : VB + 1]).astype(BF)
        for kind in range(3):
            start = (2 * kind + index) * BLK
            wq_back[:, start : start + BLK] = jnp.transpose(weight[kind * BLK : (kind + 1) * BLK])
        wp_back[rows, :] = proj
    heads[3, :, :] = dot(wp_back[...], cot_full[...]).astype(BF)
    key_place = lax.broadcasted_iota(jnp.int32, (PIX, BLK), 0)
    inside = ((key_place >> 5) < extent(ids, image, 0)) & (
        (key_place & (SIDE - 1)) < extent(ids, image, 1)
    )
    bias[...] = jnp.where(inside, 0.0, -1e30)

    def one_half(head, half):
        rows = window(head, HEAD)
        keys = heads[1, rows, :]
        values = heads[2, rows, :]
        span = window(half, BLOCK)
        query = heads[0, rows, span]
        grad = heads[3, rows, span]
        scores = dot(jnp.transpose(keys), query) + bias[:, :1]
        peak = jnp.max(scores, axis=0, keepdims=True)
        exponent = jnp.exp(scores - peak)
        inverse = 1.0 / jnp.sum(exponent, axis=0, keepdims=True)
        weights = (exponent * inverse).astype(BF)
        out = dot(values, weights)
        attended[rows, span] = out.astype(BF)
        row_term = jnp.sum(grad.astype(F32) * out, axis=0, keepdims=True)
        grad_probs = dot(jnp.transpose(values), grad)
        grad_scores = ((exponent * inverse) * (grad_probs - row_term)).astype(BF)
        grads[0, rows, span] = (dot(keys, grad_scores) * (1.0 / HEAD**0.5)).astype(BF)
        grad_vt[half] = dot(weights, jnp.transpose(grad))
        grad_kt[half] = dot(grad_scores, jnp.transpose(query))

    def one_head(head):
        loop(PIX // BLOCK, lambda half: one_half(head, half))
        rows = window(head, HEAD)
        grads[1, rows, :] = jnp.transpose(grad_kt[0] + grad_kt[1]).astype(BF)
        grads[2, rows, :] = jnp.transpose(grad_vt[0] + grad_vt[1]).astype(BF)

    loop(4, one_head)
    total[...] = dot(wq_back[...], grads[...].reshape(6 * BLK, PIX))
    split_rows(place, total, keep_norm, (give_norm0, give_norm1))


def split_rows(place, total, keep, gives):
    for index, (bit, give) in enumerate(zip((0, 2), gives)):
        rows = slice(index * BLK, (index + 1) * BLK)
        keep[rows, :] = total[block_rows(place, bit), :]
        give[...] = total[block_rows(place, bit ^ 1), :].astype(BF)


def project_kernel(ids, wp_own, half_x, half_y, attended, keep, give0, give1, total, both):
    both[:, :BLK] = wp_own[...]
    across = jnp.where((ids[1] & 1) == 1, half_x[BLK:, :], half_y[BLK:, :])
    both[:, BLK:] = jnp.transpose(across)
    total[...] = dot(both[...], attended[...])
    split_rows(ids[0], total, keep, (give0, give1))


def output_kernel(middle, keep, beside0, beside1, pack, own, across):
    for index, (bit, beside, out) in enumerate(((0, beside0, own), (2, beside1, across))):
        rows = slice(index * BLK, (index + 1) * BLK)
        cols = columns_of(pack[bit])
        total = keep[rows, :] + beside[...].astype(F32)
        out[...] = (middle[rows, :] + (total + cols[:, PB : PB + 1])).astype(BF)


def split_half(ids, bit, total, send, keep):
    half = total.shape[0] // 2
    mine = (ids[1] >> bit) & 1
    send[...] = total[window(1 - mine, half), :].astype(BF)
    keep[...] = total[window(mine, half), :].astype(keep.dtype)


EIGHTH = 4 * BLK // 8


def attend_weights_kernel(bit):
    def kernel(
        ids,
        norm_full,
        cot_full,
        attended,
        grads,
        norm_sums,
        send,
        keep,
        vec_own,
        vec_across,
        both,
    ):
        ones = jnp.ones((8, PIX), BF)
        for index, vectors in enumerate((vec_own, vec_across)):
            rows = slice(index * BLK, (index + 1) * BLK)
            for kind in range(4):
                lhs = attended[rows, :] if kind == 3 else grads[kind, rows, :]
                rhs = cot_full if kind == 3 else norm_full
                made = dot_nt(lhs, rhs[...]).astype(BF)
                for part in range(2):
                    start = (2 * (kind % 2) + part) * 2 * EIGHTH + index * EIGHTH
                    both[kind // 2, start : start + EIGHTH, :] = made[
                        part * EIGHTH : (part + 1) * EIGHTH
                    ]
            vectors[0:2, :] = norm_sums[8 * index : 8 * index + 2, :]
            vectors[2:3, :] = dot_nt(ones, grads[0, rows, :])[:1]
            vectors[3:4, :] = dot_nt(ones, grads[2, rows, :])[:1]
            vectors[4:8, :] = jnp.zeros((4, BLK), F32)
        mine = (ids[1] >> bit) & 1
        send[...] = both[1 - mine]
        keep[...] = both[mine]

    return kernel


def middle_back_kernel(
    ids, middle, keep, beside0, beside1, c0, c2, pack, branch0, branch1, sums
):
    image = image_index(ids, 0)
    mask = valid_row(ids, image)
    count = counted(ids, image)
    tops = (c0[:, image_lanes(image)], jnp.concatenate([c2[:BLK, :], c2[BLK:, :]], axis=1))
    for index, (cot, bit, beside, branch) in enumerate(
        zip(tops, (0, 2), (beside0, beside1), (branch0, branch1))
    ):
        rows = slice(index * BLK, (index + 1) * BLK)
        cols = columns_of(pack[bit])
        normal, scale = normalize(middle[rows, :], mask, count)
        upstream = keep[rows, :] + beside[...].astype(F32)
        back, with_norm, plain = norm_back(
            upstream, normal, scale[:, :1], mask, count, cols[:, GN3G : GN3G + 1]
        )
        branch[...] = (cot.astype(F32) + back).astype(BF)
        sums[8 * index : 8 * index + 8, :] = jnp.transpose(side_by_side([with_norm, plain]))[:8, :]


def branch_rows(place, pieces, full, flip):
    for bit, piece in zip((0, 2, 1, 3), pieces):
        full[block_rows(place, bit ^ (2 * flip)), :] = piece[...]


def hidden_back(ids, other, w2t, nrm2, scale2, pack, mod_ref, hidden_grad, sums, full, parts):
    image = image_index(ids, other)
    mask = valid_row(ids, image)
    count = counted(ids, image)
    parts[...] = dot(w2t[...], full[...])
    upstream = shift_sum(parts, -1)
    cols = columns_of(pack[0])
    mod = columns_of(mod_ref[image])
    gain = cols[:, GN2G : GN2G + 1]
    offset = cols[:, GN2B : GN2B + 1]
    factor = 1.0 + mod[:, 0:1]
    normal = nrm2[...]
    mixed = (normal * gain + offset) * factor + mod[:, 1:2]
    grad = upstream * silu_slope(mixed)
    plain_raw = jnp.sum(grad, axis=1, keepdims=True)
    norm_raw = jnp.sum(grad * normal, axis=1, keepdims=True)
    with_norm, plain = factor * norm_raw, factor * plain_raw
    first = group_total(gain * plain) / count
    second = group_total(gain * with_norm) / count
    back = scale2[:, :1] * ((gain * factor) * grad - mask * (first + normal * second))
    rounded = back.astype(BF)
    hidden_grad[...] = rounded
    scale_grad = gain * norm_raw + offset * plain_raw
    bias_grad = jnp.sum(rounded.astype(F32), axis=1, keepdims=True)
    columns = side_by_side([scale_grad, plain_raw, with_norm, plain, bias_grad])
    sums[...] = jnp.transpose(columns)[:8, :]


def back_own_kernel(
    ids,
    b0,
    b1,
    b2,
    b3,
    w2t,
    nrm2,
    scale2,
    pack,
    mod_ref,
    act,
    hidden_grad,
    sums,
    total,
    full,
    parts,
    stack,
):
    branch_rows(ids[0], (b0, b1, b2, b3), full, 0)
    hidden_back(ids, 0, w2t, nrm2, scale2, pack, mod_ref, hidden_grad, sums, full, parts)
    shift_stack(act, stack, 1)
    total[...] = dot_nt(full[...], stack[...])


def back_oth_kernel(
    ids,
    b0,
    b1,
    b2,
    b3,
    w2t,
    nrm2,
    scale2,
    pack,
    mod_ref,
    act,
    own,
    hidden_grad,
    sums,
    send,
    keep,
    full,
    parts,
    stack,
    total,
):
    branch_rows(ids[0], (b0, b1, b2, b3), full, 1)
    shift_stack(act, stack, 1)
    total[...] = own[...] + dot_nt(full[...], stack[...])
    split_half(ids, 0, total, send, keep)
    hidden_back(ids, 1, w2t, nrm2, scale2, pack, mod_ref, hidden_grad, sums, full, parts)


def conv1_own_kernel(grad, act, total, stack):
    shift_stack(grad, stack, -1)
    total[...] = dot_nt(stack[...], act[...])


def conv1_oth_kernel(bit):
    def kernel(ids, own, grad, act, send, keep, stack, total):
        shift_stack(grad, stack, -1)
        total[...] = own[...] + dot_nt(stack[...], act[...])
        split_half(ids, bit, total, send, keep)

    return kernel


def act_back_kernel(h_own, h_oth, w1t, keep, g00, g01, g10, g11, stack):
    for image, (ref, gives) in enumerate(((h_own, (g00, g01)), (h_oth, (g10, g11)))):
        shift_stack(ref, stack, -1)
        made = dot(w1t[...], stack[...])
        keep[:, image * PIX : (image + 1) * PIX] = made[: 2 * BLK].astype(BF)
        for index, give in enumerate(gives):
            give[...] = made[(2 + index) * BLK : (3 + index) * BLK].astype(BF)


def act_sum_kernel(keep, b00, b01, b10, b11, own, across):
    for image, (first, second) in enumerate(((b00, b01), (b10, b11))):
        lanes = slice(image * PIX, (image + 1) * PIX)
        own[:, lanes] = keep[:BLK, lanes].astype(F32) + first[...].astype(F32)
        across[:, lanes] = (keep[BLK:, lanes].astype(F32) + second[...].astype(F32)).astype(BF)


def features_back_kernel(
    ids, features, own, across, br_own, br_oth, pack, out, sums
):
    cols = columns_of(pack[0])
    gain = cols[:, GN1G : GN1G + 1]
    offset = cols[:, GN1B : GN1B + 1]
    total_norm = total_plain = total_branch = 0.0
    for block, branch in enumerate((br_own, br_oth)):
        image = image_index(ids, block)
        here = slice(block * PIX, (block + 1) * PIX)
        other = slice((1 - block) * PIX, (2 - block) * PIX)
        lanes = image_lanes(image)
        mask = valid_row(ids, image)
        count = counted(ids, image)
        normal, scale = normalize(features[:, lanes].astype(F32), mask, count)
        upstream = own[:, here] + across[:, other].astype(F32)
        grad = upstream * silu_slope(normal * gain + offset)
        back, with_norm, plain = norm_back(grad, normal, scale[:, :1], mask, count, gain)
        top = branch[...].astype(F32)
        out[:, lanes] = top + back
        total_norm = total_norm + with_norm
        total_plain = total_plain + plain
        total_branch = total_branch + jnp.sum(top, axis=1, keepdims=True)
    sums[...] = jnp.transpose(side_by_side([total_norm, total_plain, total_branch]))[:8, :]


def embed_back_kernel(ids, hsum_own, hsum_oth, emb_w, mine, beside, flat, made):
    first = ids[0] >> 1
    for kind in range(2):
        own, oth = hsum_own[kind : kind + 1, :], hsum_oth[kind : kind + 1, :]
        lanes = slice(kind * BLK, (kind + 1) * BLK)
        flat[0:1, lanes] = jnp.where(first == 0, own, oth)
        flat[1:2, lanes] = jnp.where(first == 0, oth, own)
    flat[2:8, :] = jnp.zeros((6, 2 * BLK), F32)
    rounded = flat[...].astype(BF)
    flat[...] = rounded.astype(F32)
    made[...] = dot_nt(rounded, emb_w[...])
    width = mine.shape[1]
    for bit, (out, rows) in enumerate(((mine, 0), (beside, 0), (mine, 8), (beside, 8))):
        lanes = pl.ds(pl.multiple_of((ids[0] ^ bit) * width, width), width)
        out[rows : rows + 8, :] = made[:, lanes]


def embed_across_kernel(mine, came, vec_across, out):
    out[0:8, :] = mine[8:16, :] + came[8:16, :]
    out[8:16, :] = jnp.zeros((8, out.shape[1]), F32)
    out[8:16, :BLK] = vec_across[...]


def collect_kernel(
    labels,
    fsum,
    hsum_own,
    hsum_oth,
    vec_own,
    cot_cols,
    emb_full,
    embedding,
    flat,
    mine,
    beside,
    across,
    small,
    time_grad,
):
    small[...] = jnp.zeros(small.shape, F32)
    small[0:3, :] = fsum[0:3, :]
    small[3:6, :] = hsum_own[2:5, :] + hsum_oth[2:5, :]
    small[6:10, :] = vec_own[0:4, :] + across[8:12, :BLK]
    small[10:11, :] = jnp.transpose(cot_cols[...])[0:1, :]
    came = mine[0:8, :] + beside[0:8, :] + across[0:8, :]
    grad = came[:2] * silu_slope(embedding[...])
    time_grad[...] = grad
    row = 11
    for value in (emb_full[:2, :], grad, flat[:2, :]):
        for image in range(2):
            for part in range(value.shape[1] // BLK):
                small[row : row + 1, :] = value[image : image + 1, part * BLK : (part + 1) * BLK]
                row += 1
    for image in range(2):
        label = labels[image].astype(F32)
        small[row : row + 1, :] = jnp.full((1, BLK), 1.0, F32) * label
        row += 1


def finish_kernel(ids, every, vectors, emb, time, grad, label):
    vectors[...] = jnp.zeros(vectors.shape, F32)
    for device in range(every.shape[0]):
        turn = ids[1] ^ device
        here = (turn & -8) | ((turn & 1) << 2) | (turn & 2) | ((turn >> 2) & 1)
        vectors[0:11, :] += every[here, 0:11, :]
        row = 11
        for out in (emb, time, grad, label):
            for image in range(2):
                place = slice(2 * device + image, 2 * device + image + 1)
                for part in range(out.shape[1] // BLK):
                    out[place, part * BLK : (part + 1) * BLK] = every[here, row : row + 1, :]
                    row += 1


def eighth_rows(ids, index, rows):
    mine = sum(((ids[1] >> bit) & 1) << (2 - bit) for bit in range(3))
    return pl.ds(pl.multiple_of((mine ^ index) * rows, rows), rows)


def place_conv1_kernel(ids, near, far, out):
    rows = near.shape[0] // 4
    for index in range(8):
        half = (near, far)[index // 4]
        start = (index % 4) * rows
        out[eighth_rows(ids, index, rows), :] = half[start : start + rows, :].astype(F32)


def place_conv2_kernel(ids, near, far, out):
    rows = near.shape[0] // 4
    for index in range(8):
        half = (near, far)[index // 4]
        start = (index % 4) * rows
        piece = half[start : start + rows, :].astype(F32)
        for tap in range(TAPS):
            out[tap, eighth_rows(ids, index, rows), :] = piece[:, tap * BLK : (tap + 1) * BLK]


def place_attend_kernel(ids, near, far, qkv_out, proj_out, whole):
    place_conv1_kernel(ids, near, far, whole)
    for kind in range(3):
        qkv_out[kind, :, :] = whole[kind * BLK : (kind + 1) * BLK, :]
    proj_out[...] = jnp.transpose(whole[3 * BLK :, :])


def chan_swap(value, bit):
    return lax.ppermute(value, "chan", [(place, place ^ bit) for place in range(4)])


def batch_swap(value, mask):
    size = lax.axis_size("batch")
    return lax.ppermute(value, "batch", [(place, place ^ mask) for place in range(size)])


def batch_bits():
    return lax.axis_size("batch").bit_length() - 1


class Line:
    def __init__(self, last):
        self.last = last

    def step(self, make, *values):
        values = lax.optimization_barrier((*values, self.last))[:-1]
        made = make(*values)
        self.last = made[0] if isinstance(made, tuple) else made
        return made

    def kernel(self, *args, also=(), **kwargs):
        made = call(*args, after=[self.last, *also], **kwargs)
        self.last = made[0]
        return made


def halved(index, bit):
    def make(keep, came):
        half = keep.shape[0] // 2
        mine = (index >> bit) & 1

        def part(which):
            return (
                lax.dynamic_slice_in_dim(keep, which * half, half, 0).astype(F32)
                + lax.dynamic_slice_in_dim(came, which * half, half, 0).astype(F32)
            ).astype(BF)

        return part(1 - mine), part(mine)

    return make


def added(keep, came):
    total = (keep.astype(F32) + came.astype(F32)).astype(BF)
    for bit in range(3, batch_bits()):
        total = (total.astype(F32) + batch_swap(total, 1 << bit).astype(F32)).astype(BF)
    return total


def added_pair(near, far):
    return (near.astype(F32) + far.astype(F32)).astype(BF)


def joined(*parts):
    return jnp.concatenate(parts, axis=0)


def body(
    features,
    time_emb,
    labels,
    extents,
    cotangent,
    gn1_gain,
    gn1_bias,
    conv1_w,
    conv1_b,
    emb_w,
    emb_b,
    gn2_gain,
    gn2_bias,
    conv2_w,
    conv2_b,
    gn3_gain,
    gn3_bias,
    qkv_w,
    qkv_b,
    proj_w,
    proj_b,
    class_table,
):
    place = lax.axis_index("chan").astype(jnp.int32)
    chip = place >> 1
    batch = lax.axis_index("batch").astype(jnp.int32)
    ids = jnp.concatenate([jnp.stack([place, batch]), extents.reshape(-1)])
    images = extents.shape[0]
    emb_loc = time_emb.shape[1]
    emb_rows = images * emb_loc // BLK

    def row(vector):
        return vector.reshape(1, BLK)

    across_f = chan_swap(features, 2)
    beside_f = chan_swap(features, 1)
    pack_own, embedding, crossing, cot_cols = call(
        embed_kernel,
        "embed",
        [
            ids,
            labels,
            time_emb,
            class_table,
            row(gn1_gain),
            row(gn1_bias),
            row(conv1_b),
            row(gn2_gain),
            row(gn2_bias),
            row(conv2_b),
            row(gn3_gain),
            row(gn3_bias),
            qkv_b,
            row(proj_b),
            qkv_w,
            proj_w,
            cotangent,
        ],
        [
            ((16, BLK), F32),
            ((images, emb_loc), F32),
            ((4 * BLK, PIX // 2), BF),
            ((BLK, BLK), F32),
        ],
        us=2.0,
    )
    packs = [pack_own] + [chan_swap(pack_own, bit) for bit in (1, 2, 3)]
    emb_flat = emb_w.reshape(emb_w.shape[0], -1)
    acts_near = call(
        near_kernel,
        "near",
        [ids, features, beside_f, *packs[:2]],
        [((2 * BLK, images * PIX), BF)],
        after=[emb_flat],
        us=3.0,
    )[0]
    place_late, _ = lax.optimization_barrier((place, acts_near))
    ids = ids + (place_late - place)
    emb_b_late = emb_b + (place_late - place).astype(F32)
    across_f, ids, emb_b_late, *packs[2:] = lax.optimization_barrier(
        (across_f, ids, emb_b_late, *packs[2:])
    )
    diag_f = chan_swap(across_f, 1)

    crossing, _ = lax.optimization_barrier((crossing, across_f))
    crossed = chan_swap(crossing, 2)
    half_x, cot2 = crossed[: 2 * BLK], crossed[2 * BLK :]
    half_y = batch_swap(half_x, 1)
    cot1 = chan_swap(cotangent, 1)
    pack, mod, emb_full = call(
        modulate_kernel,
        "modulate",
        [ids, *packs, emb_flat, emb_b_late],
        [((4, 16, BLK), F32), ((images, 8, BLK), F32), ((8, 4 * emb_loc), F32)],
        after=[across_f],
        us=0.3,
    )

    w1 = conv1_w.reshape(TAPS * BLK, -1)

    def front(other, after):
        return call(
            front_kernel(other),
            "front",
            [ids, acts_near, across_f, diag_f, pack, mod, w1],
            [((4 * BLK, PIX), BF), ((BLK, PIX), F32), ((BLK, BLK), F32), ((BLK, PIX), BF)],
            [((TAPS * BLK, PIX), F32), ((2, BLK, PIX), F32)],
            after=after,
            us=0.3,
        )

    def second_conv(act2, kept, after):
        return call(
            second_conv_kernel,
            "second_conv",
            [ids, conv2_w, act2],
            [((2 * BLK, PIX), kept)] + [((HALF, PIX), BF)] * 4,
            [
                ((TAPS * BLK, PIX), BF),
                ((4 * BLK, TAPS * BLK), BF),
            ],
            after=after,
            us=0.3,
        )

    act1_oth, nrm2_oth, scale2_oth, act2_oth = front(1, ())
    keep_oth, *gives = second_conv(act2_oth, BF, ())
    beside_oth = [chan_swap(give, 1) for give in gives]
    w1t, w2t = call(
        flip_kernel,
        "flip",
        [ids, conv1_w, conv2_w],
        [((4 * BLK, TAPS * BLK), BF), ((TAPS * BLK, 4 * BLK), BF)],
        after=[gives[0]],
        us=0.3,
    )
    across_sum = call(
        pair_sum_kernel,
        "pair_sum",
        [keep_oth, *beside_oth],
        [((2 * BLK, PIX), BF)],
        us=0.1,
    )[0]
    across_late, _ = lax.optimization_barrier((across_sum, crossed))
    across = chan_swap(across_late, 2)
    act1_own, nrm2_own, scale2_own, act2_own = front(0, (across_sum, w1t))
    cot2, _ = lax.optimization_barrier((cot2, act2_own))
    cot3 = chan_swap(cot2, 1)
    keep_own, *gives = second_conv(act2_own, F32, (half_y,))

    middle, normed0, normed1 = call(
        middle_kernel,
        "middle",
        [
            ids,
            keep_own,
            *[chan_swap(give, 1) for give in gives],
            across,
            features,
            across_f,
            pack,
        ],
        [((2 * BLK, PIX), F32), ((BLK, PIX), BF), ((BLK, PIX), BF)],
        us=3.0,
    )
    norm1, norm3 = chan_swap(normed0, 1), chan_swap(normed1, 1)

    norm_full, cot_full, attended, grads, keep_norm, *give_norm = call(
        attend_kernel,
        "attend",
        [
            ids,
            normed0,
            norm1,
            normed1,
            norm3,
            cotangent,
            cot1,
            cot2,
            cot3,
            pack,
            qkv_w,
            proj_w,
            half_x,
            half_y,
        ],
        [
            ((4 * BLK, PIX), BF),
            ((4 * BLK, PIX), BF),
            ((2 * BLK, PIX), BF),
            ((3, 2 * BLK, PIX), BF),
            ((2 * BLK, PIX), F32),
            ((BLK, PIX), BF),
            ((BLK, PIX), BF),
        ],
        [
            ((4, 2 * BLK, PIX), BF),
            ((4 * BLK, PIX), F32),
            ((PIX, BLK), F32),
            ((2, PIX, HEAD), F32),
            ((2, PIX, HEAD), F32),
            ((4 * BLK, 6 * BLK), BF),
            ((2 * BLK, 4 * BLK), BF),
            ((2, 2 * BLK, 4 * BLK), BF),
        ],
        us=22.0,
    )
    norm_grad_beside = [chan_swap(give, 1) for give in give_norm]
    keep_proj, *give_proj = call(
        project_kernel,
        "project",
        [ids, proj_w, half_x, half_y, attended],
        [((2 * BLK, PIX), F32), ((BLK, PIX), BF), ((BLK, PIX), BF)],
        [((4 * BLK, PIX), F32), ((4 * BLK, 2 * BLK), BF)],
        us=3.0,
    )
    proj_beside = [chan_swap(give, 1) for give in give_proj]
    branch0, branch1, norm_sums = call(
        middle_back_kernel,
        "middle_back",
        [ids, middle, keep_norm, *norm_grad_beside, cotangent, cot2, pack],
        [((BLK, PIX), BF), ((BLK, PIX), BF), ((16, BLK), F32)],
        after=[give_proj[0]],
        us=3.5,
    )
    across0, across1 = chan_swap(branch0, 2), chan_swap(branch1, 2)
    br_own = [branch0, branch1, chan_swap(branch0, 1), chan_swap(branch1, 1)]

    aw_send, aw_keep, vec_own, vec_across = call(
        attend_weights_kernel(0),
        "attend_weights",
        [ids, norm_full, cot_full, attended, grads, norm_sums],
        [
            ((4 * BLK, 4 * BLK), BF),
            ((4 * BLK, 4 * BLK), BF),
            ((8, BLK), F32),
            ((8, BLK), F32),
        ],
        [((2, 4 * BLK, 4 * BLK), BF)],
        after=[branch0],
        us=6.0,
    )
    aw_first = batch_swap(aw_send, 1)
    line = Line(aw_send)

    back_scratch = [
        ((4 * BLK, PIX), BF),
        ((TAPS * BLK, PIX), F32),
        ((TAPS * BLK, PIX), BF),
    ]
    hid_own, hsum_own, conv2_own = line.kernel(
        back_own_kernel,
        "back_own",
        [ids, *br_own, w2t, nrm2_own, scale2_own, pack, mod, act2_own],
        [((BLK, PIX), BF), ((8, BLK), F32), ((4 * BLK, TAPS * BLK), F32)],
        back_scratch,
        us=3.0,
    )
    conv1_own = line.kernel(
        conv1_own_kernel,
        "conv1_own",
        [hid_own, act1_own],
        [((TAPS * BLK, 4 * BLK), F32)],
        [((TAPS * BLK, PIX), BF)],
        us=2.0,
    )[0]
    across0, across1, _ = lax.optimization_barrier((across0, across1, conv1_own))
    br_oth = [across0, across1, chan_swap(across0, 1), chan_swap(across1, 1)]
    out_own, out_peer = line.kernel(
        output_kernel,
        "output",
        [middle, keep_proj, *proj_beside, pack],
        [((BLK, PIX), BF), ((BLK, PIX), BF)],
        also=[across1],
        us=1.0,
    )
    hid_oth, hsum_oth, conv2_send, conv2_keep = line.kernel(
        back_oth_kernel,
        "back_oth",
        [ids, *br_oth, w2t, nrm2_oth, scale2_oth, pack, mod, act2_oth, conv2_own],
        [
            ((BLK, PIX), BF),
            ((8, BLK), F32),
            ((2 * BLK, TAPS * BLK), BF),
            ((2 * BLK, TAPS * BLK), BF),
        ],
        back_scratch + [((4 * BLK, TAPS * BLK), F32)],
        us=0.5,
    )
    conv1_send, conv1_keep = line.kernel(
        conv1_oth_kernel(0),
        "conv1_oth",
        [ids, conv1_own, hid_oth, act1_oth],
        [((TAPS * BLK // 2, 4 * BLK), BF), ((TAPS * BLK // 2, 4 * BLK), BF)],
        [((TAPS * BLK, PIX), BF), ((TAPS * BLK, 4 * BLK), F32)],
        also=[aw_first],
        us=0.5,
    )
    aw_send, aw_keep = line.step(halved(batch, 1), aw_keep, aw_first)
    aw_send, aw_keep = line.step(halved(batch, 2), aw_keep, batch_swap(aw_send, 2))
    conv2_send, conv2_keep = line.step(
        halved(batch, 1), conv2_keep, batch_swap(conv2_send, 1)
    )
    keep_act, *give_act = line.kernel(
        act_back_kernel,
        "act_back",
        [hid_own, hid_oth, w1t],
        [((2 * BLK, 2 * PIX), BF)] + [((BLK, PIX), BF)] * 4,
        [((TAPS * BLK, PIX), BF)],
        us=0.5,
    )
    aw_part = line.step(added, aw_keep, batch_swap(aw_send, 4))
    conv2_send, conv2_keep = line.step(
        halved(batch, 2), conv2_keep, batch_swap(conv2_send, 2)
    )
    conv1_send, conv1_keep = line.step(
        halved(batch, 1), conv1_keep, batch_swap(conv1_send, 1)
    )
    act_own, act_send = line.kernel(
        act_sum_kernel,
        "act_sum",
        [keep_act, *[chan_swap(give, 1) for give in give_act]],
        [((BLK, 2 * PIX), F32), ((BLK, 2 * PIX), BF)],
        us=0.1,
    )
    act_across = chan_swap(act_send, 2)
    emb_mine, emb_give, flat_embed = line.kernel(
        embed_back_kernel,
        "embed_back",
        [ids, hsum_own, hsum_oth, emb_flat],
        [((16, emb_loc), F32), ((16, emb_loc), F32), ((8, 2 * BLK), F32)],
        [((8, 4 * emb_loc), F32)],
        us=0.1,
    )
    emb_beside = chan_swap(emb_give, 1)
    aw_near = line.step(added_pair, aw_part[:EIGHTH], chan_swap(aw_part[EIGHTH:], 2))
    conv2_near = line.step(added, conv2_keep, batch_swap(conv2_send, 4))
    emb_send = line.kernel(
        embed_across_kernel,
        "embed_across",
        [emb_mine, emb_beside, vec_across],
        [((16, emb_loc), F32)],
        us=0.1,
    )[0]
    emb_across = chan_swap(emb_send, 2)
    conv1_send, conv1_keep = line.step(
        halved(batch, 2), conv1_keep, batch_swap(conv1_send, 2)
    )
    aw_near = line.step(joined, aw_near, batch_swap(aw_near, 4))
    conv2_near = line.step(joined, conv2_near, batch_swap(conv2_near, 4))
    aw_near = line.step(joined, aw_near, batch_swap(aw_near, 2))
    conv1_near = line.step(added, conv1_keep, batch_swap(conv1_send, 4))
    features_grad, fsum = line.kernel(
        features_back_kernel,
        "features_back",
        [ids, features, act_own, act_across, branch0, across1, pack],
        [((BLK, 2 * PIX), F32), ((8, BLK), F32)],
        us=0.1,
    )
    conv2_near = line.step(joined, conv2_near, batch_swap(conv2_near, 2))
    ends = np.cumsum([11, images * 4 * emb_loc // BLK, emb_rows, images * 2, images])
    small, time_grad = line.kernel(
        collect_kernel,
        "collect",
        [
            labels,
            fsum,
            hsum_own,
            hsum_oth,
            vec_own,
            cot_cols,
            emb_full,
            embedding,
            flat_embed,
            emb_mine,
            emb_beside,
            emb_across,
        ],
        [(((int(ends[-1]) + 7) // 8 * 8, BLK), F32), ((images, emb_loc), F32)],
        us=0.1,
    )
    conv1_near = line.step(joined, conv1_near, batch_swap(conv1_near, 4))
    qkv_w_grad, proj_w_grad = line.kernel(
        place_attend_kernel,
        "place_attend",
        [ids, aw_near, batch_swap(aw_near, 1)],
        [((3, BLK, 4 * BLK), F32), ((4 * BLK, BLK), F32)],
        [((4 * BLK, 4 * BLK), F32)],
        us=0.1,
    )
    every = small[None]
    if batch_bits() > 2:
        every = line.step(joined, every, batch_swap(every, 4))
    every = line.step(joined, every, batch_swap(every, 2))
    conv2_w_grad = line.kernel(
        place_conv2_kernel,
        "place_conv2",
        [ids, conv2_near, batch_swap(conv2_near, 1)],
        [((TAPS, 4 * BLK, BLK), F32)],
        us=0.1,
    )[0]
    conv1_near = line.step(joined, conv1_near, batch_swap(conv1_near, 2))
    every = line.step(joined, every, batch_swap(every, 1))
    for bit in range(3, batch_bits()):
        every = line.step(joined, every, batch_swap(every, 1 << bit))

    devices = every.shape[0]
    vectors, every_emb, every_time, every_grad, every_label = line.kernel(
        finish_kernel,
        "finish",
        [ids, every],
        [
            ((16, BLK), F32),
            ((devices * images, 4 * emb_loc), F32),
            ((devices * images, emb_loc), F32),
            ((devices * images, 2 * BLK), F32),
            ((devices * images, BLK), F32),
        ],
        us=0.1,
    )
    every_label = every_label[:, 0].astype(jnp.int32)
    emb_w_grad = lax.dot_general(
        every_emb.astype(BF),
        every_grad.astype(BF),
        (((0,), (0,)), ((), ())),
        preferred_element_type=F32,
    ).reshape(emb_w.shape)
    emb_b_grad = jnp.sum(every_grad, axis=0).reshape(emb_b.shape)
    onehot = (jnp.arange(CLASSES, dtype=jnp.int32)[:, None] == every_label[None, :]).astype(F32)
    class_table_grad = jnp.dot(onehot, every_time, precision=highest)

    out_late, _ = lax.optimization_barrier((out_peer, conv1_near))
    out_across = chan_swap(out_late, 2)
    output = jnp.where(
        chip == 0,
        jnp.concatenate([out_own, out_across], axis=1),
        jnp.concatenate([out_across, out_own], axis=1),
    )
    conv1_w_grad = line.kernel(
        place_conv1_kernel,
        "place_conv1",
        [ids, conv1_near, batch_swap(conv1_near, 1)],
        [((TAPS * BLK, 4 * BLK), F32)],
        us=0.5,
    )[0].reshape(conv1_w.shape)
    return (
        output,
        features_grad,
        time_grad,
        vectors[0],
        vectors[1],
        conv1_w_grad,
        vectors[5],
        emb_w_grad,
        emb_b_grad,
        vectors[3],
        vectors[4],
        conv2_w_grad,
        vectors[2],
        vectors[6],
        vectors[7],
        qkv_w_grad,
        vectors[8:10],
        proj_w_grad,
        vectors[10],
        class_table_grad,
    )


def solution(mesh):
    placed = (
        P("chan", "batch"),
        P("batch", "chan"),
        P("batch"),
        P("batch", None),
        P("chan", "batch"),
        P("chan"),
        P("chan"),
        P(None, "chan", None),
        P("chan"),
        P(None, None, "chan"),
        P(None, "chan"),
        P("chan"),
        P("chan"),
        P(None, None, "chan"),
        P("chan"),
        P("chan"),
        P("chan"),
        P(None, "chan", None),
        P(None, "chan"),
        P(None, "chan"),
        P("chan"),
        P(None, "chan"),
    )
    return jax.shard_map(
        body,
        mesh=mesh,
        in_specs=placed,
        out_specs=(
            P("chan", "batch"),
            P("chan", "batch"),
            P("batch", "chan"),
            P("chan"),
            P("chan"),
            P(None, "chan", None),
            P("chan"),
            P(None, None, "chan"),
            P(None, "chan"),
            P("chan"),
            P("chan"),
            P(None, None, "chan"),
            P("chan"),
            P("chan"),
            P("chan"),
            P(None, "chan", None),
            P(None, "chan"),
            P(None, "chan"),
            P("chan"),
            P(None, "chan"),
        ),
        check_vma=False,
    )
```

```python
import jax
import jax.numpy as jnp
import numpy as np
from jax import lax
from jax.experimental import pallas as pl
from jax.experimental.pallas import tpu as pltpu
from jax.sharding import PartitionSpec as P

CLASSES = 1000
SIDE = 32
PIX = SIDE * SIDE
BLK = 128
HEAD = 64
HALF = BLK // 2
WIDTH = 16
TAPS = 9
BF = jnp.bfloat16
F32 = jnp.float32
highest = lax.Precision.HIGHEST

GN1G, GN1B, C1B, GN2G, GN2B, C2B, GN3G, GN3B, QB, VB, PB, EMB0 = range(12)


def call(kernel, name, inputs, outs, scratch=(), after=(), us=2.0):
    smem = pl.BlockSpec(memory_space=pltpu.SMEM)
    vmem = pl.BlockSpec(memory_space=pltpu.VMEM)
    specs = [smem if value.dtype == jnp.int32 else vmem for value in inputs]
    specs += [pl.BlockSpec(memory_space=pl.ANY)] * len(after)
    first, last = len(inputs), len(inputs) + len(after)

    def body_of(*refs):
        kernel(*refs[:first], *refs[last:])

    return pl.pallas_call(
        body_of,
        name=name,
        out_shape=[jax.ShapeDtypeStruct(shape, dtype) for shape, dtype in outs],
        in_specs=specs,
        out_specs=[vmem] * len(outs),
        scratch_shapes=[pltpu.VMEM(shape, dtype) for shape, dtype in scratch],
        compiler_params=pltpu.CompilerParams(vmem_limit_bytes=MIB[name] * 2**20),
        cost_estimate=pl.CostEstimate(
            flops=0, bytes_accessed=int(us * COST_PER_US), transcendentals=0
        ),
    )(*inputs, *after)


COST_PER_US = 3_000_000
MIB = dict(
    embed=64,
    near=64,
    modulate=6,
    front=24,
    second_conv=16,
    pair_sum=4,
    flip=8,
    middle=12,
    attend=32,
    project=10,
    middle_back=12,
    attend_weights=12,
    back_own=24,
    back_oth=28,
    output=8,
    conv1_own=20,
    conv1_oth=20,
    act_back=16,
    act_sum=8,
    embed_back=6,
    embed_across=4,
    features_back=12,
    collect=4,
    finish=4,
    place_conv1=10,
    place_conv2=10,
    place_attend=8,
)


def dot(lhs, rhs):
    return jnp.dot(lhs, rhs, preferred_element_type=F32)


def dot_nt(lhs, rhs):
    return lax.dot_general(lhs, rhs, (((1,), (1,)), ((), ())), preferred_element_type=F32)


def loop(count, step):
    def body_of(index, carry):
        step(index)
        return carry

    lax.fori_loop(0, count, body_of, 0)


def window(index, size):
    return pl.ds(pl.multiple_of(index * size, size), size)


def pixel_rows():
    place = lax.broadcasted_iota(jnp.int32, (1, PIX), 1)
    return place >> 5, place & (SIDE - 1)


def image_index(ids, other):
    return (ids[0] >> 1) ^ other


def extent(ids, image, axis):
    return ids[2 + 2 * image + axis]


def valid_row(ids, image):
    row, col = pixel_rows()
    inside = (row < extent(ids, image, 0)) & (col < extent(ids, image, 1))
    return jnp.where(inside, 1.0, 0.0).astype(F32)


def counted(ids, image):
    return (WIDTH * extent(ids, image, 0) * extent(ids, image, 1)).astype(F32)


def normalize(values, mask, count):
    channels = values.shape[0]
    grouped = values.reshape(channels // WIDTH, WIDTH, PIX)
    weight = mask.reshape(1, 1, PIX)
    center = jnp.sum(grouped * weight, axis=(1, 2), keepdims=True) / count
    deviate = grouped - center
    spread = jnp.sum(deviate * deviate * weight, axis=(1, 2), keepdims=True) / count
    scale = lax.rsqrt(spread + 1e-05)
    normal = (deviate * scale).reshape(channels, PIX)
    spread_out = jnp.broadcast_to(scale, (channels // WIDTH, WIDTH, BLK)).reshape(channels, BLK)
    return normal, spread_out


def group_total(column):
    channels = column.shape[0]
    wide = jnp.broadcast_to(column, (channels, BLK)).reshape(channels // WIDTH, WIDTH, BLK)
    summed = jnp.sum(wide, axis=1, keepdims=True)
    return jnp.broadcast_to(summed, wide.shape).reshape(channels, BLK)[:, :1]


def norm_back(upstream, normal, scale, mask, count, gain):
    with_norm = jnp.sum(upstream * normal, axis=1, keepdims=True)
    plain = jnp.sum(upstream, axis=1, keepdims=True)
    first = group_total(gain * plain) / count
    second = group_total(gain * with_norm) / count
    back = scale * (gain * upstream - mask * (first + normal * second))
    return back, with_norm, plain


def silu(value):
    half = 0.5 * value
    return half + half * jnp.tanh(half)


def silu_slope(value):
    gate = 0.5 + 0.5 * jnp.tanh(0.5 * value)
    return gate * (1.0 + value * (1.0 - gate))


def move_rows(value, step):
    row, _ = pixel_rows()
    moved = pltpu.roll(value, (-SIDE * step) % PIX, 1)
    return jnp.where((row + step >= 0) & (row + step < SIDE), moved, 0.0)


def move_cols(value, step):
    _, col = pixel_rows()
    moved = pltpu.roll(value, (-step) % PIX, 1)
    return jnp.where((col + step >= 0) & (col + step < SIDE), moved, 0.0)


def tap_start(row_step, col_step):
    return (3 * (row_step + 1) + col_step + 1) * BLK


def tap_rows(row_step, col_step):
    start = tap_start(row_step, col_step)
    return slice(start, start + BLK)


def shift_sum(parts, direction):
    total = None
    for col_step in (-1, 0, 1):
        column = parts[tap_rows(0, col_step), :]
        for row_step in (-1, 1):
            column = column + move_rows(parts[tap_rows(row_step, col_step), :], direction * row_step)
        if col_step:
            column = move_cols(column, direction * col_step)
        total = column if total is None else total + column
    return total


def shift_stack(value, stack, direction):
    whole = value[...].astype(F32)
    for row_step in (-1, 0, 1):
        row_moved = whole if row_step == 0 else move_rows(whole, direction * row_step)
        for col_step in (-1, 0, 1):
            moved = row_moved if col_step == 0 else move_cols(row_moved, direction * col_step)
            stack[tap_rows(row_step, col_step), :] = moved.astype(BF)


def block_rows(place, bit):
    return pl.ds(pl.multiple_of((place ^ bit) * BLK, BLK), BLK)


def image_lanes(image):
    return pl.ds(pl.multiple_of(image * PIX, PIX), PIX)


def columns_of(rows):
    return jnp.transpose(rows)


def side_by_side(columns):
    channels = columns[0].shape[0]
    lane = lax.broadcasted_iota(jnp.int32, (channels, BLK), 1)
    wide = jnp.zeros((channels, BLK), F32)
    for index, column in enumerate(columns):
        wide = jnp.where(lane == index, column, wide)
    return wide


def embed_kernel(
    ids,
    labels,
    time_emb,
    table,
    g1,
    b1,
    c1,
    g2,
    b2,
    c2,
    g3,
    b3,
    qvb,
    pb,
    qkv,
    proj,
    cot,
    pack,
    embedding,
    crossing,
    cot_cols,
):
    for part in range(2):
        start = image_index(ids, 1) * PIX + part * PIX // 2
        crossing[(2 + part) * BLK : (3 + part) * BLK, :] = cot[
            :, pl.ds(pl.multiple_of(start, PIX // 2), PIX // 2)
        ]
    cot_cols[...] = jnp.broadcast_to(
        jnp.sum(cot[...].astype(F32), axis=1, keepdims=True), (BLK, BLK)
    )

    @pl.when((ids[1] & 1) == 0)
    def _():
        crossing[:BLK, :] = qkv[0]
        crossing[BLK : 2 * BLK, :] = qkv[1]

    @pl.when((ids[1] & 1) == 1)
    def _():
        crossing[:BLK, :] = qkv[2]
        crossing[BLK : 2 * BLK, :] = jnp.transpose(proj[...])

    width = time_emb.shape[1]
    for row, ref in enumerate((g1, b1, c1, g2, b2, c2, g3, b3)):
        pack[row : row + 1, :] = ref[...]
    pack[QB : QB + 2, :] = qvb[...]
    pack[PB : PB + 1, :] = pb[...]
    pack[EMB0 + 4 :, :] = jnp.zeros((1, BLK), F32)
    kind = lax.broadcasted_iota(jnp.int32, (16, CLASSES), 1)
    row = lax.broadcasted_iota(jnp.int32, (16, CLASSES), 0)
    label = jnp.where(row == 0, labels[0], labels[1])
    rows = dot(jnp.where((kind == label) & (row < 2), 1.0, 0.0).astype(BF), table[...])
    total = time_emb[...].astype(F32) + rows[:2]
    embedding[...] = total
    act = silu(total).astype(BF).astype(F32)
    for image in range(2):
        for part in range(width // BLK):
            place = EMB0 + image * (width // BLK) + part
            pack[place : place + 1, :] = act[
                image : image + 1, part * BLK : (part + 1) * BLK
            ]


def first_act(feat, cols, mask, count):
    normal, _ = normalize(feat.astype(F32), mask, count)
    return silu(normal * cols[:, GN1G : GN1G + 1] + cols[:, GN1B : GN1B + 1]).astype(BF)


def near_kernel(ids, f0, f1, p0, p1, acts):
    for block, (feat, pack) in enumerate(((f0, p0), (f1, p1))):
        cols = columns_of(pack[...])

        def step(image):
            lanes = image_lanes(image)
            acts[block * BLK : (block + 1) * BLK, lanes] = first_act(
                feat[:, lanes], cols, valid_row(ids, image), counted(ids, image)
            )

        loop(2, step)


def modulate_kernel(ids, p0, p1, p2, p3, emb_w, emb_b, pack, mod, emb_full):
    for bit, ref in enumerate((p0, p1, p2, p3)):
        pack[bit] = ref[...]
    width = emb_full.shape[1] // 4
    emb_full[...] = jnp.zeros(emb_full.shape, F32)
    for bit in range(4):
        for image in range(2):
            for part in range(width // BLK):
                row = EMB0 + image * (width // BLK) + part
                lanes = pl.ds(pl.multiple_of((ids[0] ^ bit) * width + part * BLK, BLK), BLK)
                emb_full[image : image + 1, lanes] = pack[bit, row : row + 1, :]
    made = dot(emb_full[...].astype(BF), emb_w[...])
    mod[...] = jnp.zeros(mod.shape, F32)
    for image in range(2):
        for kind in range(2):
            mod[image, kind : kind + 1, :] = (
                made[image : image + 1, kind * BLK : (kind + 1) * BLK] + emb_b[kind : kind + 1, :]
            )


def front_kernel(other):
    def kernel(
        ids, near, f2, f3, pack, mod_ref, w1, act1, nrm2, scale2, act2, parts, hidden
    ):
        place = ids[0]
        image = image_index(ids, other)
        lanes = image_lanes(image)
        mask = valid_row(ids, image)
        count = counted(ids, image)
        for bit in (0, 1):
            act1[block_rows(place, bit), :] = near[bit * BLK : (bit + 1) * BLK, lanes]
        hidden[0] = f2[:, lanes].astype(F32)
        hidden[1] = f3[:, lanes].astype(F32)

        def first(block):
            cols = columns_of(pack[2 + block])
            act1[block_rows(place, 2 + block), :] = first_act(hidden[block], cols, mask, count)

        loop(2, first)
        parts[...] = dot(w1[...], act1[...])
        cols = columns_of(pack[0])
        normal, scale = normalize(shift_sum(parts, 1) + cols[:, C1B : C1B + 1], mask, count)
        nrm2[...] = normal
        scale2[...] = scale
        mod = columns_of(mod_ref[image])
        plain = normal * cols[:, GN2G : GN2G + 1] + cols[:, GN2B : GN2B + 1]
        act2[...] = silu(plain * (1.0 + mod[:, 0:1]) + mod[:, 1:2]).astype(BF)

    return kernel


def second_conv_kernel(ids, w2, act2, keep, g0, g1, g2, g3, stack, w2_rows):
    place = ids[0]
    for slot, bit in enumerate((0, 2, 1, 3)):
        for tap in range(TAPS):
            w2_rows[slot * BLK : (slot + 1) * BLK, tap * BLK : (tap + 1) * BLK] = w2[
                tap, block_rows(place, bit), :
            ]
    shift_stack(act2, stack, 1)
    made = dot(w2_rows[...], stack[...])
    keep[...] = made[: 2 * BLK].astype(keep.dtype)
    for index, give in enumerate((g0, g1, g2, g3)):
        start = 2 * BLK + index * HALF
        give[...] = made[start : start + HALF].astype(BF)


def pair_sum_kernel(keep, b0, b1, b2, b3, out):
    for index, beside in enumerate((b0, b1, b2, b3)):
        rows = slice(index * HALF, (index + 1) * HALF)
        out[rows, :] = (keep[rows, :].astype(F32) + beside[...].astype(F32)).astype(BF)


def flip_kernel(ids, w1, w2, w1t, w2t):
    place = ids[0]

    def step(tap):
        lanes = window(tap, BLK)
        for slot, bit in enumerate((0, 2, 1, 3)):
            block = w1[tap, :, block_rows(place, bit)]
            w1t[slot * BLK : (slot + 1) * BLK, lanes] = jnp.transpose(block)
        w2t[lanes, :] = jnp.transpose(w2[tap])

    loop(TAPS, step)


def middle_kernel(
    ids, keep, b0, b1, b2, b3, across, f0, f2, pack, middle, normed0, normed1
):
    image = image_index(ids, 0)
    mask = valid_row(ids, image)
    count = counted(ids, image)
    feats = (f0[:, image_lanes(image)], f2[:, image_lanes(image)])
    for index, (feat, pieces, bit, normed) in enumerate(
        zip(feats, ((b0, b1), (b2, b3)), (0, 2), (normed0, normed1))
    ):
        rows = slice(index * BLK, (index + 1) * BLK)
        other = slice((1 - index) * BLK, (2 - index) * BLK)
        cols = columns_of(pack[bit])
        beside = jnp.concatenate([piece[...].astype(F32) for piece in pieces], axis=0)
        total = keep[rows, :] + beside + across[other, :].astype(F32)
        total = feat.astype(F32) + (total + cols[:, C2B : C2B + 1])
        middle[rows, :] = total
        normal, _ = normalize(total, mask, count)
        normed[...] = (normal * cols[:, GN3G : GN3G + 1] + cols[:, GN3B : GN3B + 1]).astype(BF)


BLOCK = 512


def attend_kernel(
    ids,
    norm0,
    norm1,
    norm2,
    norm3,
    c0,
    c1,
    c2,
    c3,
    pack,
    wq_own,
    wp_own,
    half_x,
    half_y,
    norm_full,
    cot_full,
    attended,
    grads,
    keep_norm,
    give_norm0,
    give_norm1,
    heads,
    total,
    bias,
    grad_kt,
    grad_vt,
    wq_back,
    wp_back,
    across,
):
    place = ids[0]
    image = image_index(ids, 0)
    mine = ids[1] & 1
    across[mine] = half_x[...]
    across[1 - mine] = half_y[...]
    wq_across = across[...].reshape(4 * BLK, 4 * BLK)
    for bit, ref in enumerate((norm0, norm1, norm2, norm3)):
        norm_full[block_rows(place, bit), :] = ref[...]
    for bit, ref in enumerate((c0, c1)):
        cot_full[block_rows(place, bit), :] = ref[:, image_lanes(image)]
    for bit, ref in enumerate((c2, c3)):
        for part in range(2):
            lanes = slice(part * PIX // 2, (part + 1) * PIX // 2)
            cot_full[block_rows(place, bit + 2), lanes] = ref[part * BLK : (part + 1) * BLK, :]
    cols_own = columns_of(pack[0])
    cols_across = columns_of(pack[2])
    own = wq_own[...].reshape(3 * BLK, 4 * BLK)
    for index, (weight, proj, cols) in enumerate(
        (
            (own, jnp.transpose(wp_own[...]), cols_own),
            (wq_across[: 3 * BLK], wq_across[3 * BLK :], cols_across),
        )
    ):
        rows = slice(index * BLK, (index + 1) * BLK)
        made = dot(weight, norm_full[...])
        query = (made[:BLK] + cols[:, QB : QB + 1]).astype(BF)
        heads[0, rows, :] = (query.astype(F32) * (1.0 / HEAD**0.5)).astype(BF)
        heads[1, rows, :] = made[BLK : 2 * BLK].astype(BF)
        heads[2, rows, :] = (made[2 * BLK :] + cols[:, VB : VB + 1]).astype(BF)
        for kind in range(3):
            start = (2 * kind + index) * BLK
            wq_back[:, start : start + BLK] = jnp.transpose(weight[kind * BLK : (kind + 1) * BLK])
        wp_back[rows, :] = proj
    heads[3, :, :] = dot(wp_back[...], cot_full[...]).astype(BF)
    key_place = lax.broadcasted_iota(jnp.int32, (PIX, BLK), 0)
    inside = ((key_place >> 5) < extent(ids, image, 0)) & (
        (key_place & (SIDE - 1)) < extent(ids, image, 1)
    )
    bias[...] = jnp.where(inside, 0.0, -1e30)

    def one_half(head, half):
        rows = window(head, HEAD)
        keys = heads[1, rows, :]
        values = heads[2, rows, :]
        span = window(half, BLOCK)
        query = heads[0, rows, span]
        grad = heads[3, rows, span]
        scores = dot(jnp.transpose(keys), query) + bias[:, :1]
        peak = jnp.max(scores, axis=0, keepdims=True)
        exponent = jnp.exp(scores - peak)
        inverse = 1.0 / jnp.sum(exponent, axis=0, keepdims=True)
        weights = (exponent * inverse).astype(BF)
        out = dot(values, weights)
        attended[rows, span] = out.astype(BF)
        row_term = jnp.sum(grad.astype(F32) * out, axis=0, keepdims=True)
        grad_probs = dot(jnp.transpose(values), grad)
        grad_scores = ((exponent * inverse) * (grad_probs - row_term)).astype(BF)
        grads[0, rows, span] = (dot(keys, grad_scores) * (1.0 / HEAD**0.5)).astype(BF)
        grad_vt[half] = dot(weights, jnp.transpose(grad))
        grad_kt[half] = dot(grad_scores, jnp.transpose(query))

    def one_head(head):
        loop(PIX // BLOCK, lambda half: one_half(head, half))
        rows = window(head, HEAD)
        grads[1, rows, :] = jnp.transpose(grad_kt[0] + grad_kt[1]).astype(BF)
        grads[2, rows, :] = jnp.transpose(grad_vt[0] + grad_vt[1]).astype(BF)

    loop(4, one_head)
    total[...] = dot(wq_back[...], grads[...].reshape(6 * BLK, PIX))
    split_rows(place, total, keep_norm, (give_norm0, give_norm1))


def split_rows(place, total, keep, gives):
    for index, (bit, give) in enumerate(zip((0, 2), gives)):
        rows = slice(index * BLK, (index + 1) * BLK)
        keep[rows, :] = total[block_rows(place, bit), :]
        give[...] = total[block_rows(place, bit ^ 1), :].astype(BF)


def project_kernel(ids, wp_own, half_x, half_y, attended, keep, give0, give1, total, both):
    both[:, :BLK] = wp_own[...]
    across = jnp.where((ids[1] & 1) == 1, half_x[BLK:, :], half_y[BLK:, :])
    both[:, BLK:] = jnp.transpose(across)
    total[...] = dot(both[...], attended[...])
    split_rows(ids[0], total, keep, (give0, give1))


def output_kernel(middle, keep, beside0, beside1, pack, own, across):
    for index, (bit, beside, out) in enumerate(((0, beside0, own), (2, beside1, across))):
        rows = slice(index * BLK, (index + 1) * BLK)
        cols = columns_of(pack[bit])
        total = keep[rows, :] + beside[...].astype(F32)
        out[...] = (middle[rows, :] + (total + cols[:, PB : PB + 1])).astype(BF)


def split_half(ids, bit, total, send, keep):
    half = total.shape[0] // 2
    mine = (ids[1] >> bit) & 1
    send[...] = total[window(1 - mine, half), :].astype(BF)
    keep[...] = total[window(mine, half), :].astype(keep.dtype)


EIGHTH = 4 * BLK // 8


def attend_weights_kernel(bit):
    def kernel(
        ids,
        norm_full,
        cot_full,
        attended,
        grads,
        norm_sums,
        send,
        keep,
        vec_own,
        vec_across,
        both,
    ):
        ones = jnp.ones((8, PIX), BF)
        for index, vectors in enumerate((vec_own, vec_across)):
            rows = slice(index * BLK, (index + 1) * BLK)
            for kind in range(4):
                lhs = attended[rows, :] if kind == 3 else grads[kind, rows, :]
                rhs = cot_full if kind == 3 else norm_full
                made = dot_nt(lhs, rhs[...]).astype(BF)
                for part in range(2):
                    start = (2 * (kind % 2) + part) * 2 * EIGHTH + index * EIGHTH
                    both[kind // 2, start : start + EIGHTH, :] = made[
                        part * EIGHTH : (part + 1) * EIGHTH
                    ]
            vectors[0:2, :] = norm_sums[8 * index : 8 * index + 2, :]
            vectors[2:3, :] = dot_nt(ones, grads[0, rows, :])[:1]
            vectors[3:4, :] = dot_nt(ones, grads[2, rows, :])[:1]
            vectors[4:8, :] = jnp.zeros((4, BLK), F32)
        mine = (ids[1] >> bit) & 1
        send[...] = both[1 - mine]
        keep[...] = both[mine]

    return kernel


def middle_back_kernel(
    ids, middle, keep, beside0, beside1, c0, c2, pack, branch0, branch1, sums
):
    image = image_index(ids, 0)
    mask = valid_row(ids, image)
    count = counted(ids, image)
    tops = (c0[:, image_lanes(image)], jnp.concatenate([c2[:BLK, :], c2[BLK:, :]], axis=1))
    for index, (cot, bit, beside, branch) in enumerate(
        zip(tops, (0, 2), (beside0, beside1), (branch0, branch1))
    ):
        rows = slice(index * BLK, (index + 1) * BLK)
        cols = columns_of(pack[bit])
        normal, scale = normalize(middle[rows, :], mask, count)
        upstream = keep[rows, :] + beside[...].astype(F32)
        back, with_norm, plain = norm_back(
            upstream, normal, scale[:, :1], mask, count, cols[:, GN3G : GN3G + 1]
        )
        branch[...] = (cot.astype(F32) + back).astype(BF)
        sums[8 * index : 8 * index + 8, :] = jnp.transpose(side_by_side([with_norm, plain]))[:8, :]


def branch_rows(place, pieces, full, flip):
    for bit, piece in zip((0, 2, 1, 3), pieces):
        full[block_rows(place, bit ^ (2 * flip)), :] = piece[...]


def hidden_back(ids, other, w2t, nrm2, scale2, pack, mod_ref, hidden_grad, sums, full, parts):
    image = image_index(ids, other)
    mask = valid_row(ids, image)
    count = counted(ids, image)
    parts[...] = dot(w2t[...], full[...])
    upstream = shift_sum(parts, -1)
    cols = columns_of(pack[0])
    mod = columns_of(mod_ref[image])
    gain = cols[:, GN2G : GN2G + 1]
    offset = cols[:, GN2B : GN2B + 1]
    factor = 1.0 + mod[:, 0:1]
    normal = nrm2[...]
    mixed = (normal * gain + offset) * factor + mod[:, 1:2]
    grad = upstream * silu_slope(mixed)
    plain_raw = jnp.sum(grad, axis=1, keepdims=True)
    norm_raw = jnp.sum(grad * normal, axis=1, keepdims=True)
    with_norm, plain = factor * norm_raw, factor * plain_raw
    first = group_total(gain * plain) / count
    second = group_total(gain * with_norm) / count
    back = scale2[:, :1] * ((gain * factor) * grad - mask * (first + normal * second))
    rounded = back.astype(BF)
    hidden_grad[...] = rounded
    scale_grad = gain * norm_raw + offset * plain_raw
    bias_grad = jnp.sum(rounded.astype(F32), axis=1, keepdims=True)
    columns = side_by_side([scale_grad, plain_raw, with_norm, plain, bias_grad])
    sums[...] = jnp.transpose(columns)[:8, :]


def back_own_kernel(
    ids,
    b0,
    b1,
    b2,
    b3,
    w2t,
    nrm2,
    scale2,
    pack,
    mod_ref,
    act,
    hidden_grad,
    sums,
    total,
    full,
    parts,
    stack,
):
    branch_rows(ids[0], (b0, b1, b2, b3), full, 0)
    hidden_back(ids, 0, w2t, nrm2, scale2, pack, mod_ref, hidden_grad, sums, full, parts)
    shift_stack(act, stack, 1)
    total[...] = dot_nt(full[...], stack[...])


def back_oth_kernel(
    ids,
    b0,
    b1,
    b2,
    b3,
    w2t,
    nrm2,
    scale2,
    pack,
    mod_ref,
    act,
    own,
    hidden_grad,
    sums,
    send,
    keep,
    full,
    parts,
    stack,
    total,
):
    branch_rows(ids[0], (b0, b1, b2, b3), full, 1)
    shift_stack(act, stack, 1)
    total[...] = own[...] + dot_nt(full[...], stack[...])
    split_half(ids, 0, total, send, keep)
    hidden_back(ids, 1, w2t, nrm2, scale2, pack, mod_ref, hidden_grad, sums, full, parts)


def conv1_own_kernel(grad, act, total, stack):
    shift_stack(grad, stack, -1)
    total[...] = dot_nt(stack[...], act[...])


def conv1_oth_kernel(bit):
    def kernel(ids, own, grad, act, send, keep, stack, total):
        shift_stack(grad, stack, -1)
        total[...] = own[...] + dot_nt(stack[...], act[...])
        split_half(ids, bit, total, send, keep)

    return kernel


def act_back_kernel(h_own, h_oth, w1t, keep, g00, g01, g10, g11, stack):
    for image, (ref, gives) in enumerate(((h_own, (g00, g01)), (h_oth, (g10, g11)))):
        shift_stack(ref, stack, -1)
        made = dot(w1t[...], stack[...])
        keep[:, image * PIX : (image + 1) * PIX] = made[: 2 * BLK].astype(BF)
        for index, give in enumerate(gives):
            give[...] = made[(2 + index) * BLK : (3 + index) * BLK].astype(BF)


def act_sum_kernel(keep, b00, b01, b10, b11, own, across):
    for image, (first, second) in enumerate(((b00, b01), (b10, b11))):
        lanes = slice(image * PIX, (image + 1) * PIX)
        own[:, lanes] = keep[:BLK, lanes].astype(F32) + first[...].astype(F32)
        across[:, lanes] = (keep[BLK:, lanes].astype(F32) + second[...].astype(F32)).astype(BF)


def features_back_kernel(
    ids, features, own, across, br_own, br_oth, pack, out, sums
):
    cols = columns_of(pack[0])
    gain = cols[:, GN1G : GN1G + 1]
    offset = cols[:, GN1B : GN1B + 1]
    total_norm = total_plain = total_branch = 0.0
    for block, branch in enumerate((br_own, br_oth)):
        image = image_index(ids, block)
        here = slice(block * PIX, (block + 1) * PIX)
        other = slice((1 - block) * PIX, (2 - block) * PIX)
        lanes = image_lanes(image)
        mask = valid_row(ids, image)
        count = counted(ids, image)
        normal, scale = normalize(features[:, lanes].astype(F32), mask, count)
        upstream = own[:, here] + across[:, other].astype(F32)
        grad = upstream * silu_slope(normal * gain + offset)
        back, with_norm, plain = norm_back(grad, normal, scale[:, :1], mask, count, gain)
        top = branch[...].astype(F32)
        out[:, lanes] = top + back
        total_norm = total_norm + with_norm
        total_plain = total_plain + plain
        total_branch = total_branch + jnp.sum(top, axis=1, keepdims=True)
    sums[...] = jnp.transpose(side_by_side([total_norm, total_plain, total_branch]))[:8, :]


def embed_back_kernel(ids, hsum_own, hsum_oth, emb_w, mine, beside, flat, made):
    first = ids[0] >> 1
    for kind in range(2):
        own, oth = hsum_own[kind : kind + 1, :], hsum_oth[kind : kind + 1, :]
        lanes = slice(kind * BLK, (kind + 1) * BLK)
        flat[0:1, lanes] = jnp.where(first == 0, own, oth)
        flat[1:2, lanes] = jnp.where(first == 0, oth, own)
    flat[2:8, :] = jnp.zeros((6, 2 * BLK), F32)
    rounded = flat[...].astype(BF)
    flat[...] = rounded.astype(F32)
    made[...] = dot_nt(rounded, emb_w[...])
    width = mine.shape[1]
    for bit, (out, rows) in enumerate(((mine, 0), (beside, 0), (mine, 8), (beside, 8))):
        lanes = pl.ds(pl.multiple_of((ids[0] ^ bit) * width, width), width)
        out[rows : rows + 8, :] = made[:, lanes]


def embed_across_kernel(mine, came, vec_across, out):
    out[0:8, :] = mine[8:16, :] + came[8:16, :]
    out[8:16, :] = jnp.zeros((8, out.shape[1]), F32)
    out[8:16, :BLK] = vec_across[...]


def collect_kernel(
    labels,
    fsum,
    hsum_own,
    hsum_oth,
    vec_own,
    cot_cols,
    emb_full,
    embedding,
    flat,
    mine,
    beside,
    across,
    small,
    time_grad,
):
    small[...] = jnp.zeros(small.shape, F32)
    small[0:3, :] = fsum[0:3, :]
    small[3:6, :] = hsum_own[2:5, :] + hsum_oth[2:5, :]
    small[6:10, :] = vec_own[0:4, :] + across[8:12, :BLK]
    small[10:11, :] = jnp.transpose(cot_cols[...])[0:1, :]
    came = mine[0:8, :] + beside[0:8, :] + across[0:8, :]
    grad = came[:2] * silu_slope(embedding[...])
    time_grad[...] = grad
    row = 11
    for value in (emb_full[:2, :], grad, flat[:2, :]):
        for image in range(2):
            for part in range(value.shape[1] // BLK):
                small[row : row + 1, :] = value[image : image + 1, part * BLK : (part + 1) * BLK]
                row += 1
    for image in range(2):
        label = labels[image].astype(F32)
        small[row : row + 1, :] = jnp.full((1, BLK), 1.0, F32) * label
        row += 1


def finish_kernel(ids, every, vectors, emb, time, grad, label):
    vectors[...] = jnp.zeros(vectors.shape, F32)
    for device in range(every.shape[0]):
        turn = ids[1] ^ device
        here = (turn & -8) | ((turn & 1) << 2) | (turn & 2) | ((turn >> 2) & 1)
        vectors[0:11, :] += every[here, 0:11, :]
        row = 11
        for out in (emb, time, grad, label):
            for image in range(2):
                place = slice(2 * device + image, 2 * device + image + 1)
                for part in range(out.shape[1] // BLK):
                    out[place, part * BLK : (part + 1) * BLK] = every[here, row : row + 1, :]
                    row += 1


def eighth_rows(ids, index, rows):
    mine = sum(((ids[1] >> bit) & 1) << (2 - bit) for bit in range(3))
    return pl.ds(pl.multiple_of((mine ^ index) * rows, rows), rows)


def place_conv1_kernel(ids, near, far, out):
    rows = near.shape[0] // 4
    for index in range(8):
        half = (near, far)[index // 4]
        start = (index % 4) * rows
        out[eighth_rows(ids, index, rows), :] = half[start : start + rows, :].astype(F32)


def place_conv2_kernel(ids, near, far, out):
    rows = near.shape[0] // 4
    for index in range(8):
        half = (near, far)[index // 4]
        start = (index % 4) * rows
        piece = half[start : start + rows, :].astype(F32)
        for tap in range(TAPS):
            out[tap, eighth_rows(ids, index, rows), :] = piece[:, tap * BLK : (tap + 1) * BLK]


def place_attend_kernel(ids, near, far, qkv_out, proj_out, whole):
    place_conv1_kernel(ids, near, far, whole)
    for kind in range(3):
        qkv_out[kind, :, :] = whole[kind * BLK : (kind + 1) * BLK, :]
    proj_out[...] = jnp.transpose(whole[3 * BLK :, :])


def chan_swap(value, bit):
    return lax.ppermute(value, "chan", [(place, place ^ bit) for place in range(4)])


def batch_swap(value, mask):
    size = lax.axis_size("batch")
    return lax.ppermute(value, "batch", [(place, place ^ mask) for place in range(size)])


def batch_bits():
    return lax.axis_size("batch").bit_length() - 1


class Line:
    def __init__(self, last):
        self.last = last

    def step(self, make, *values):
        values = lax.optimization_barrier((*values, self.last))[:-1]
        made = make(*values)
        self.last = made[0] if isinstance(made, tuple) else made
        return made

    def kernel(self, *args, also=(), **kwargs):
        made = call(*args, after=[self.last, *also], **kwargs)
        self.last = made[0]
        return made


def halved(index, bit):
    def make(keep, came):
        half = keep.shape[0] // 2
        mine = (index >> bit) & 1

        def part(which):
            return (
                lax.dynamic_slice_in_dim(keep, which * half, half, 0).astype(F32)
                + lax.dynamic_slice_in_dim(came, which * half, half, 0).astype(F32)
            ).astype(BF)

        return part(1 - mine), part(mine)

    return make


def added(keep, came):
    total = (keep.astype(F32) + came.astype(F32)).astype(BF)
    for bit in range(3, batch_bits()):
        total = (total.astype(F32) + batch_swap(total, 1 << bit).astype(F32)).astype(BF)
    return total


def added_pair(near, far):
    return (near.astype(F32) + far.astype(F32)).astype(BF)


def joined(*parts):
    return jnp.concatenate(parts, axis=0)


def body(
    features,
    time_emb,
    labels,
    extents,
    cotangent,
    gn1_gain,
    gn1_bias,
    conv1_w,
    conv1_b,
    emb_w,
    emb_b,
    gn2_gain,
    gn2_bias,
    conv2_w,
    conv2_b,
    gn3_gain,
    gn3_bias,
    qkv_w,
    qkv_b,
    proj_w,
    proj_b,
    class_table,
):
    place = lax.axis_index("chan").astype(jnp.int32)
    chip = place >> 1
    batch = lax.axis_index("batch").astype(jnp.int32)
    ids = jnp.concatenate([jnp.stack([place, batch]), extents.reshape(-1)])
    images = extents.shape[0]
    emb_loc = time_emb.shape[1]
    emb_rows = images * emb_loc // BLK

    def row(vector):
        return vector.reshape(1, BLK)

    across_f = chan_swap(features, 2)
    beside_f = chan_swap(features, 1)
    pack_own, embedding, crossing, cot_cols = call(
        embed_kernel,
        "embed",
        [
            ids,
            labels,
            time_emb,
            class_table,
            row(gn1_gain),
            row(gn1_bias),
            row(conv1_b),
            row(gn2_gain),
            row(gn2_bias),
            row(conv2_b),
            row(gn3_gain),
            row(gn3_bias),
            qkv_b,
            row(proj_b),
            qkv_w,
            proj_w,
            cotangent,
        ],
        [
            ((16, BLK), F32),
            ((images, emb_loc), F32),
            ((4 * BLK, PIX // 2), BF),
            ((BLK, BLK), F32),
        ],
        us=2.0,
    )
    packs = [pack_own] + [chan_swap(pack_own, bit) for bit in (1, 2, 3)]
    emb_flat = emb_w.reshape(emb_w.shape[0], -1)
    acts_near = call(
        near_kernel,
        "near",
        [ids, features, beside_f, *packs[:2]],
        [((2 * BLK, images * PIX), BF)],
        after=[emb_flat],
        us=3.0,
    )[0]
    place_late, _ = lax.optimization_barrier((place, acts_near))
    ids = ids + (place_late - place)
    emb_b_late = emb_b + (place_late - place).astype(F32)
    across_f, *packs[2:], _ = lax.optimization_barrier((across_f, *packs[2:], acts_near))
    diag_f = chan_swap(across_f, 1)

    crossing, _ = lax.optimization_barrier((crossing, across_f))
    crossed = chan_swap(crossing, 2)
    half_x, cot2 = crossed[: 2 * BLK], crossed[2 * BLK :]
    half_y = batch_swap(half_x, 1)
    cot1 = chan_swap(cotangent, 1)
    pack, mod, emb_full = call(
        modulate_kernel,
        "modulate",
        [ids, *packs, emb_flat, emb_b_late],
        [((4, 16, BLK), F32), ((images, 8, BLK), F32), ((8, 4 * emb_loc), F32)],
        after=[across_f],
        us=0.3,
    )

    w1 = conv1_w.reshape(TAPS * BLK, -1)

    def front(other, after):
        return call(
            front_kernel(other),
            "front",
            [ids, acts_near, across_f, diag_f, pack, mod, w1],
            [((4 * BLK, PIX), BF), ((BLK, PIX), F32), ((BLK, BLK), F32), ((BLK, PIX), BF)],
            [((TAPS * BLK, PIX), F32), ((2, BLK, PIX), F32)],
            after=after,
            us=0.3,
        )

    def second_conv(act2, kept, after):
        return call(
            second_conv_kernel,
            "second_conv",
            [ids, conv2_w, act2],
            [((2 * BLK, PIX), kept)] + [((HALF, PIX), BF)] * 4,
            [
                ((TAPS * BLK, PIX), BF),
                ((4 * BLK, TAPS * BLK), BF),
            ],
            after=after,
            us=0.3,
        )

    act1_oth, nrm2_oth, scale2_oth, act2_oth = front(1, ())
    keep_oth, *gives = second_conv(act2_oth, BF, ())
    beside_oth = [chan_swap(give, 1) for give in gives]
    w1t, w2t = call(
        flip_kernel,
        "flip",
        [ids, conv1_w, conv2_w],
        [((4 * BLK, TAPS * BLK), BF), ((TAPS * BLK, 4 * BLK), BF)],
        after=[gives[0]],
        us=0.3,
    )
    across_sum = call(
        pair_sum_kernel,
        "pair_sum",
        [keep_oth, *beside_oth],
        [((2 * BLK, PIX), BF)],
        us=0.1,
    )[0]
    across_late, _ = lax.optimization_barrier((across_sum, crossed))
    across = chan_swap(across_late, 2)
    act1_own, nrm2_own, scale2_own, act2_own = front(0, (across_sum, w1t))
    cot2, _ = lax.optimization_barrier((cot2, act2_own))
    cot3 = chan_swap(cot2, 1)
    keep_own, *gives = second_conv(act2_own, F32, (half_y,))

    middle, normed0, normed1 = call(
        middle_kernel,
        "middle",
        [
            ids,
            keep_own,
            *[chan_swap(give, 1) for give in gives],
            across,
            features,
            across_f,
            pack,
        ],
        [((2 * BLK, PIX), F32), ((BLK, PIX), BF), ((BLK, PIX), BF)],
        us=3.0,
    )
    norm1, norm3 = chan_swap(normed0, 1), chan_swap(normed1, 1)

    norm_full, cot_full, attended, grads, keep_norm, *give_norm = call(
        attend_kernel,
        "attend",
        [
            ids,
            normed0,
            norm1,
            normed1,
            norm3,
            cotangent,
            cot1,
            cot2,
            cot3,
            pack,
            qkv_w,
            proj_w,
            half_x,
            half_y,
        ],
        [
            ((4 * BLK, PIX), BF),
            ((4 * BLK, PIX), BF),
            ((2 * BLK, PIX), BF),
            ((3, 2 * BLK, PIX), BF),
            ((2 * BLK, PIX), F32),
            ((BLK, PIX), BF),
            ((BLK, PIX), BF),
        ],
        [
            ((4, 2 * BLK, PIX), BF),
            ((4 * BLK, PIX), F32),
            ((PIX, BLK), F32),
            ((2, PIX, HEAD), F32),
            ((2, PIX, HEAD), F32),
            ((4 * BLK, 6 * BLK), BF),
            ((2 * BLK, 4 * BLK), BF),
            ((2, 2 * BLK, 4 * BLK), BF),
        ],
        us=22.0,
    )
    norm_grad_beside = [chan_swap(give, 1) for give in give_norm]
    keep_proj, *give_proj = call(
        project_kernel,
        "project",
        [ids, proj_w, half_x, half_y, attended],
        [((2 * BLK, PIX), F32), ((BLK, PIX), BF), ((BLK, PIX), BF)],
        [((4 * BLK, PIX), F32), ((4 * BLK, 2 * BLK), BF)],
        us=3.0,
    )
    proj_beside = [chan_swap(give, 1) for give in give_proj]
    branch0, branch1, norm_sums = call(
        middle_back_kernel,
        "middle_back",
        [ids, middle, keep_norm, *norm_grad_beside, cotangent, cot2, pack],
        [((BLK, PIX), BF), ((BLK, PIX), BF), ((16, BLK), F32)],
        after=[give_proj[0]],
        us=3.5,
    )
    across0, across1 = chan_swap(branch0, 2), chan_swap(branch1, 2)
    br_own = [branch0, branch1, chan_swap(branch0, 1), chan_swap(branch1, 1)]

    aw_send, aw_keep, vec_own, vec_across = call(
        attend_weights_kernel(0),
        "attend_weights",
        [ids, norm_full, cot_full, attended, grads, norm_sums],
        [
            ((4 * BLK, 4 * BLK), BF),
            ((4 * BLK, 4 * BLK), BF),
            ((8, BLK), F32),
            ((8, BLK), F32),
        ],
        [((2, 4 * BLK, 4 * BLK), BF)],
        after=[branch0],
        us=6.0,
    )
    aw_first = batch_swap(aw_send, 1)
    line = Line(aw_send)

    back_scratch = [
        ((4 * BLK, PIX), BF),
        ((TAPS * BLK, PIX), F32),
        ((TAPS * BLK, PIX), BF),
    ]
    hid_own, hsum_own, conv2_own = line.kernel(
        back_own_kernel,
        "back_own",
        [ids, *br_own, w2t, nrm2_own, scale2_own, pack, mod, act2_own],
        [((BLK, PIX), BF), ((8, BLK), F32), ((4 * BLK, TAPS * BLK), F32)],
        back_scratch,
        us=3.0,
    )
    conv1_own = line.kernel(
        conv1_own_kernel,
        "conv1_own",
        [hid_own, act1_own],
        [((TAPS * BLK, 4 * BLK), F32)],
        [((TAPS * BLK, PIX), BF)],
        us=2.0,
    )[0]
    across0, across1, _ = lax.optimization_barrier((across0, across1, conv1_own))
    br_oth = [across0, across1, chan_swap(across0, 1), chan_swap(across1, 1)]
    out_own, out_peer = line.kernel(
        output_kernel,
        "output",
        [middle, keep_proj, *proj_beside, pack],
        [((BLK, PIX), BF), ((BLK, PIX), BF)],
        also=[across1],
        us=1.0,
    )
    hid_oth, hsum_oth, conv2_send, conv2_keep = line.kernel(
        back_oth_kernel,
        "back_oth",
        [ids, *br_oth, w2t, nrm2_oth, scale2_oth, pack, mod, act2_oth, conv2_own],
        [
            ((BLK, PIX), BF),
            ((8, BLK), F32),
            ((2 * BLK, TAPS * BLK), BF),
            ((2 * BLK, TAPS * BLK), BF),
        ],
        back_scratch + [((4 * BLK, TAPS * BLK), F32)],
        us=0.5,
    )
    conv1_send, conv1_keep = line.kernel(
        conv1_oth_kernel(0),
        "conv1_oth",
        [ids, conv1_own, hid_oth, act1_oth],
        [((TAPS * BLK // 2, 4 * BLK), BF), ((TAPS * BLK // 2, 4 * BLK), BF)],
        [((TAPS * BLK, PIX), BF), ((TAPS * BLK, 4 * BLK), F32)],
        also=[aw_first],
        us=0.5,
    )
    aw_send, aw_keep = line.step(halved(batch, 1), aw_keep, aw_first)
    aw_send, aw_keep = line.step(halved(batch, 2), aw_keep, batch_swap(aw_send, 2))
    conv2_send, conv2_keep = line.step(
        halved(batch, 1), conv2_keep, batch_swap(conv2_send, 1)
    )
    keep_act, *give_act = line.kernel(
        act_back_kernel,
        "act_back",
        [hid_own, hid_oth, w1t],
        [((2 * BLK, 2 * PIX), BF)] + [((BLK, PIX), BF)] * 4,
        [((TAPS * BLK, PIX), BF)],
        us=0.5,
    )
    aw_part = line.step(added, aw_keep, batch_swap(aw_send, 4))
    conv2_send, conv2_keep = line.step(
        halved(batch, 2), conv2_keep, batch_swap(conv2_send, 2)
    )
    conv1_send, conv1_keep = line.step(
        halved(batch, 1), conv1_keep, batch_swap(conv1_send, 1)
    )
    act_own, act_send = line.kernel(
        act_sum_kernel,
        "act_sum",
        [keep_act, *[chan_swap(give, 1) for give in give_act]],
        [((BLK, 2 * PIX), F32), ((BLK, 2 * PIX), BF)],
        us=0.1,
    )
    act_across = chan_swap(act_send, 2)
    emb_mine, emb_give, flat_embed = line.kernel(
        embed_back_kernel,
        "embed_back",
        [ids, hsum_own, hsum_oth, emb_flat],
        [((16, emb_loc), F32), ((16, emb_loc), F32), ((8, 2 * BLK), F32)],
        [((8, 4 * emb_loc), F32)],
        us=0.1,
    )
    emb_beside = chan_swap(emb_give, 1)
    aw_near = line.step(added_pair, aw_part[:EIGHTH], chan_swap(aw_part[EIGHTH:], 2))
    conv2_near = line.step(added, conv2_keep, batch_swap(conv2_send, 4))
    emb_send = line.kernel(
        embed_across_kernel,
        "embed_across",
        [emb_mine, emb_beside, vec_across],
        [((16, emb_loc), F32)],
        us=0.1,
    )[0]
    emb_across = chan_swap(emb_send, 2)
    conv1_send, conv1_keep = line.step(
        halved(batch, 2), conv1_keep, batch_swap(conv1_send, 2)
    )
    aw_near = line.step(joined, aw_near, batch_swap(aw_near, 4))
    conv2_near = line.step(joined, conv2_near, batch_swap(conv2_near, 4))
    aw_near = line.step(joined, aw_near, batch_swap(aw_near, 2))
    conv1_near = line.step(added, conv1_keep, batch_swap(conv1_send, 4))
    features_grad, fsum = line.kernel(
        features_back_kernel,
        "features_back",
        [ids, features, act_own, act_across, branch0, across1, pack],
        [((BLK, 2 * PIX), F32), ((8, BLK), F32)],
        us=0.1,
    )
    conv2_near = line.step(joined, conv2_near, batch_swap(conv2_near, 2))
    ends = np.cumsum([11, images * 4 * emb_loc // BLK, emb_rows, images * 2, images])
    small, time_grad = line.kernel(
        collect_kernel,
        "collect",
        [
            labels,
            fsum,
            hsum_own,
            hsum_oth,
            vec_own,
            cot_cols,
            emb_full,
            embedding,
            flat_embed,
            emb_mine,
            emb_beside,
            emb_across,
        ],
        [(((int(ends[-1]) + 7) // 8 * 8, BLK), F32), ((images, emb_loc), F32)],
        us=0.1,
    )
    conv1_near = line.step(joined, conv1_near, batch_swap(conv1_near, 4))
    qkv_w_grad, proj_w_grad = line.kernel(
        place_attend_kernel,
        "place_attend",
        [ids, aw_near, batch_swap(aw_near, 1)],
        [((3, BLK, 4 * BLK), F32), ((4 * BLK, BLK), F32)],
        [((4 * BLK, 4 * BLK), F32)],
        us=0.1,
    )
    every = small[None]
    if batch_bits() > 2:
        every = line.step(joined, every, batch_swap(every, 4))
    every = line.step(joined, every, batch_swap(every, 2))
    conv2_w_grad = line.kernel(
        place_conv2_kernel,
        "place_conv2",
        [ids, conv2_near, batch_swap(conv2_near, 1)],
        [((TAPS, 4 * BLK, BLK), F32)],
        us=0.1,
    )[0]
    conv1_near = line.step(joined, conv1_near, batch_swap(conv1_near, 2))
    every = line.step(joined, every, batch_swap(every, 1))
    for bit in range(3, batch_bits()):
        every = line.step(joined, every, batch_swap(every, 1 << bit))

    devices = every.shape[0]
    vectors, every_emb, every_time, every_grad, every_label = line.kernel(
        finish_kernel,
        "finish",
        [ids, every],
        [
            ((16, BLK), F32),
            ((devices * images, 4 * emb_loc), F32),
            ((devices * images, emb_loc), F32),
            ((devices * images, 2 * BLK), F32),
            ((devices * images, BLK), F32),
        ],
        us=0.1,
    )
    every_label = every_label[:, 0].astype(jnp.int32)
    emb_w_grad = lax.dot_general(
        every_emb.astype(BF),
        every_grad.astype(BF),
        (((0,), (0,)), ((), ())),
        preferred_element_type=F32,
    ).reshape(emb_w.shape)
    emb_b_grad = jnp.sum(every_grad, axis=0).reshape(emb_b.shape)
    onehot = (jnp.arange(CLASSES, dtype=jnp.int32)[:, None] == every_label[None, :]).astype(F32)
    class_table_grad = jnp.dot(onehot, every_time, precision=highest)

    out_late, _ = lax.optimization_barrier((out_peer, conv1_near))
    out_across = chan_swap(out_late, 2)
    output = jnp.where(
        chip == 0,
        jnp.concatenate([out_own, out_across], axis=1),
        jnp.concatenate([out_across, out_own], axis=1),
    )
    conv1_w_grad = line.kernel(
        place_conv1_kernel,
        "place_conv1",
        [ids, conv1_near, batch_swap(conv1_near, 1)],
        [((TAPS * BLK, 4 * BLK), F32)],
        us=0.5,
    )[0].reshape(conv1_w.shape)
    return (
        output,
        features_grad,
        time_grad,
        vectors[0],
        vectors[1],
        conv1_w_grad,
        vectors[5],
        emb_w_grad,
        emb_b_grad,
        vectors[3],
        vectors[4],
        conv2_w_grad,
        vectors[2],
        vectors[6],
        vectors[7],
        qkv_w_grad,
        vectors[8:10],
        proj_w_grad,
        vectors[10],
        class_table_grad,
    )


def solution(mesh):
    placed = (
        P("chan", "batch"),
        P("batch", "chan"),
        P("batch"),
        P("batch", None),
        P("chan", "batch"),
        P("chan"),
        P("chan"),
        P(None, "chan", None),
        P("chan"),
        P(None, None, "chan"),
        P(None, "chan"),
        P("chan"),
        P("chan"),
        P(None, None, "chan"),
        P("chan"),
        P("chan"),
        P("chan"),
        P(None, "chan", None),
        P(None, "chan"),
        P(None, "chan"),
        P("chan"),
        P(None, "chan"),
    )
    return jax.shard_map(
        body,
        mesh=mesh,
        in_specs=placed,
        out_specs=(
            P("chan", "batch"),
            P("chan", "batch"),
            P("batch", "chan"),
            P("chan"),
            P("chan"),
            P(None, "chan", None),
            P("chan"),
            P(None, None, "chan"),
            P(None, "chan"),
            P("chan"),
            P("chan"),
            P(None, None, "chan"),
            P("chan"),
            P("chan"),
            P("chan"),
            P(None, "chan", None),
            P(None, "chan"),
            P(None, "chan"),
            P("chan"),
            P(None, "chan"),
        ),
        check_vma=False,
    )
```
